32 devices in a mesh: req: 2 (over y), exp: 16 (over z, x, core).
Axes of the slice: x: 2, y: 2, z: 4, core: 2. Of those that a mesh axis runs over, the one named last changes fastest.
Arguments:
- queries: bfloat16 [4096, 2048], P(('req', 'exp')), may hold values from -128 to 128
- keys_then_values: bfloat16 [4096, 1024], P(('req', 'exp')), may hold values from -8 to 8
- residual: bfloat16 [4096, 2048], P(('req', 'exp')), may hold values from -6 to 6
- norm_gain: bfloat16 [2048], replicated, may hold values from 0.099609375 to 1.8984375
- prompt_lengths: int32 [2, 16], P('req'), may hold values from 1 to 1536, 2048 in all within a row
- expert_ids: int32 [4096, 6], P(('req', 'exp')), may hold values from 0 to 15, all different within a row; in each aligned block of 128 rows (0 to 127, 128 to 255, ...) at most 72 rows name the same one
- router_logits: float32 [4096, 6], P(('req', 'exp')), may hold values from -10 to 320
- w_gate: bfloat16 [16, 2048, 1408], P('exp'), may hold values from -0.125 to 0.125
- w_up: bfloat16 [16, 2048, 1408], P('exp'), may hold values from -0.125 to 0.125
- w_down: bfloat16 [16, 1408, 2048], P('exp'), may hold values from -0.15625 to 0.15625
- w_shared_gate: bfloat16 [2048, 2816], P('exp', 'req'), may hold values from -0.125 to 0.125
- w_shared_up: bfloat16 [2048, 2816], P('exp', 'req'), may hold values from -0.125 to 0.125
- w_shared_down: bfloat16 [2048, 2816], P('exp', 'req'), may hold values from -0.109375 to 0.109375
- page_table: int32 [2, 128], replicated, may hold values from 0 to 255, as said below
Outputs:
- layer_out: bfloat16 [4096, 2048], P(('req', 'exp'))
- kv_cache: bfloat16 [256, 16, 1024], P(('req', 'exp'))
- log_totals: float32 [16, 4096], P(None, ('req', 'exp'))
The draws below stay inside these ranges and needn't reach their ends.
Inputs may be any that keep to these rules, and one draw needn't show every extreme that they name: `expert_ids`: in the rows of one device no expert is named more than 72 times. `page_table`: the entries are a permutation of 0 to 255. Entry [r, j] lies in the aligned block of 8 slots whose index modulo 128 // 8 equals j // 8; each aligned block of 8 entries of a row names exactly 4 slots in each aligned block of 128 slots.
All inputs are finite; a program needn't handle non-finite values.
Results may differ from the reference program's by a relative error of at most 0.0065.
Values may be sent and summed in bfloat16 or wider, within the bound.
No kernel may reach another device: no remote copies, remote signals or barrier semaphores. Data moves between devices by JAX's collectives and lax.ppermute only.
A program may use at most 192 MiB of HBM per device.

```python
import math
import jax
import jax.numpy as jnp
import numpy as np
from jax import lax

D = 2048
QUERY_HEADS = 16
KEY_VALUE_HEADS = 4
HEAD_SIZE = 128
FF = 1408
TOPK = 6
PAGE = 16
NPROMPT = 16
TOK_DEV = 128
SFF = 2816
GROUPS = 2
EXPERTS = 16
G_TOK = 2048
TOKEN_TOTAL = 4096
MAXLEN = 1536
CAP = 72
PAGES_DEV = 8
PGROUP = 4
GPAGES = 128
N_EXP = 16


def value_offsets(key):
    phase_key = jax.random.fold_in(key, 53)
    phases = jax.random.uniform(phase_key, (1, KEY_VALUE_HEADS * HEAD_SIZE), jnp.float32, -3.14159, 3.14159)
    block_index = (jnp.arange(TOKEN_TOTAL) // 128).astype(jnp.float32)
    return 2.5 * jnp.cos(2.4 * block_index[:, None] + phases)


def attention_pair(key):
    base_key = jax.random.fold_in(key, 11)
    query_key, key_value_random = jax.random.split(base_key, 2)
    offsets = value_offsets(key)
    queries = jnp.clip(jax.random.normal(query_key, (TOKEN_TOTAL, QUERY_HEADS * HEAD_SIZE), jnp.float32), -6.0, 6.0)
    key_value_rows = jnp.clip(jax.random.normal(key_value_random, (TOKEN_TOTAL, 2 * KEY_VALUE_HEADS * HEAD_SIZE), jnp.float32), -6.0, 6.0)
    value_portion = key_value_rows[:, KEY_VALUE_HEADS * HEAD_SIZE:] + offsets
    key_value_rows = jnp.concatenate([key_value_rows[:, :KEY_VALUE_HEADS * HEAD_SIZE], value_portion], axis=1)
    key_value_rows = jnp.clip(key_value_rows, -8.0, 8.0)
    return (queries, key_value_rows)


def draw_queries(key, part):
    return attention_pair(key)[0].astype(jnp.bfloat16)


def draw_keys_then_values(key, part):
    return attention_pair(key)[1].astype(jnp.bfloat16)


def draw_router_logits(key, part):
    base_key = jax.random.fold_in(key, 23)
    first_key = jax.random.fold_in(base_key, 0)
    logits = jnp.clip(1.5 * jax.random.normal(first_key, (TOKEN_TOTAL, TOPK), jnp.float32), -9.0, 9.0)
    return logits


def draw_page_table(key, part):
    base_key = jax.random.fold_in(key, 37)
    source_key, dest_key = jax.random.split(base_key)
    columns = GPAGES // PAGES_DEV
    count_all = GROUPS * columns
    sigma = jax.vmap(lambda one_key: jax.random.permutation(one_key, PAGES_DEV))(jax.random.split(source_key, count_all))
    sigma = sigma.reshape(GROUPS, columns, PAGES_DEV)
    tau_perm = jax.vmap(lambda one_key: jax.random.permutation(one_key, PAGES_DEV))(jax.random.split(dest_key, count_all))
    tau_perm = tau_perm.reshape(GROUPS, columns, PAGES_DEV)
    dest_group = sigma % GROUPS
    order_in = sigma // GROUPS
    source_group = jnp.arange(GROUPS)[:, None, None]
    column_index = jnp.arange(columns)[None, :, None]
    incoming = source_group * PGROUP + order_in
    slot_in = tau_perm[dest_group, column_index, incoming]
    global_slot = dest_group * GPAGES + column_index * PAGES_DEV + slot_in
    return global_slot.reshape(GROUPS, GPAGES).astype(jnp.int32)


def steps_of(own_key, extent, cuts, low, largest):
    factor_of = 1.0
    for axis_at, shards_of in cuts:
        heights = jax.random.uniform(jax.random.fold_in(jax.random.fold_in(own_key, 6), axis_at), (shards_of,), jnp.float32, low / len(cuts), largest / len(cuts))
        factor_of = factor_of * jnp.repeat(jnp.exp(heights), extent[axis_at] // shards_of).reshape((-1,) + (1,) * (len(extent) - 1 - axis_at))
    return factor_of


def length_profile(number_of, total, bound, slope):
    loads = [(1 << 20) // math.isqrt(grade ** slope) + 1 for grade in range(2, number_of + 1)]
    rest, holding = total - bound - (number_of - 1), [1] * (number_of - 1)
    while rest > 0:
        free = [i for i in range(number_of - 1) if holding[i] < bound]
        whole, left = sum([loads[i] for i in free]), rest
        for i in free:
            extra = min(bound - holding[i], max(1, left * loads[i] // whole), rest)
            holding[i] = holding[i] + extra
            rest = rest - extra
    return np.array([bound] + holding)


def ragged(stream_key, count, total, limit, skew):
    if count == 2:
        one = jax.random.randint(stream_key, (), max(1, total - limit), min(limit, total - 1) + 1)
        return jnp.stack([one, total - one])
    sizes = jnp.asarray(length_profile(count, total, limit, skew), jnp.int32)
    couples = (count - 1) // 2
    source_of, receiver = sizes[1:1 + 2 * couples:2], sizes[2:2 + 2 * couples:2]
    margin = jnp.minimum(source_of - 1, limit - receiver)
    passed = jax.random.randint(jax.random.fold_in(stream_key, 1), (couples,), 0, 1 << 20) % (margin + 1)
    sizes = sizes.at[1:1 + 2 * couples:2].set(source_of - passed).at[2:2 + 2 * couples:2].set(receiver + passed)
    return sizes[jax.random.permutation(jax.random.fold_in(stream_key, 2), count)]


def deal_out(own_key, own, number, rows, count, top, reach, skew):
    sequence = jax.random.permutation(own_key, count)
    crowded, usual = portions_of(count, rows * top, reach, skew, True), portions_of(count, rows * top, reach, skew, False)
    places = jnp.arange(count)

    def named(sizes, rotation):
        used = int((sizes > 0).sum())
        fixed = max(1, used // 4)
        moved = fixed + (places - fixed + rotation * (used - fixed)) % max(1, count - fixed)
        return jnp.zeros((count,), jnp.int32).at[sequence[jnp.where(places < fixed, places, moved)]].set(jnp.asarray(sizes, jnp.int32))

    sizes = jnp.where(number % 4 == 0, named(crowded, number // 4), named(usual, number - number // 4 - 1))
    mixed = jax.random.permutation(jax.random.fold_in(own, 3), count)
    source_of, sink = mixed[0:count // 2 * 2:2], mixed[1:count // 2 * 2:2]
    slack = jnp.minimum(sizes[source_of] - 1, reach - sizes[sink]) // 2
    slack = jnp.where((source_of == sequence[0]) | (sink == sequence[0]) | (sizes[sink] == 0), 0, jnp.maximum(slack, 0))
    moved = jax.random.randint(jax.random.fold_in(own, 4), (count // 2,), 0, 1 << 20) % (slack + 1)
    sizes = sizes.at[source_of].add(-moved).at[sink].add(moved)
    items = jnp.searchsorted(jnp.cumsum(sizes), jnp.arange(rows * top), side="right").astype(jnp.int32)
    grid = items.reshape(top, rows).T
    grid = grid[jax.random.permutation(jax.random.fold_in(own, 1), rows)]
    rotation = jax.random.randint(jax.random.fold_in(own, 2), (rows, 1), 0, top)
    return jnp.take_along_axis(grid, (jnp.arange(top)[None, :] + rotation) % top, axis=1)


def portions_of(count, total, reach, slope, full):
    portions = [(1 << 20) // math.isqrt(standing ** slope) + 1 for standing in range(1, count + 1)]
    largest = reach if full else min(reach, max(-(-total // count), total * portions[0] // sum(portions)))
    least = 1 if total - largest >= count - 1 else 0
    given, spare = [largest] + [least] * (count - 1), total - largest - least * (count - 1)
    while spare > 0:
        movable = [i for i in range(1, count) if given[i] < largest] or [i for i in range(1, count) if given[i] < reach]
        mass, budget = sum([portions[i] for i in movable]), spare
        for i in movable:
            more = min(reach - given[i], max(1, budget * portions[i] // mass), spare)
            given[i] = given[i] + more
            spare = spare - more
    return np.array(given)


def scatter_about(own_key, shape, scale, limit, pieces=(), kind=jnp.bfloat16):
    values = jax.random.normal(own_key, shape, jnp.float32) * scale
    if len(pieces) > 0:
        values = steps_of(own_key, shape, pieces, -0.22, 0.18) * values
    return jnp.clip(values, min=-limit, max=limit).astype(kind)


def setup_inputs(seed: int = 0) -> dict:
    key_list = jax.random.split(jax.random.key(seed), 15)
    queries = draw_queries(jax.random.fold_in(key_list[14], 71), 0)
    keys_then_values = draw_keys_then_values(jax.random.fold_in(key_list[14], 71), 0)
    residual = scatter_about(key_list[2], (TOKEN_TOTAL, D), 1.0, 6.0, ((0, 32),))
    norm_gain = jnp.clip(1.0 + 0.18 * jax.random.normal(key_list[3], (D,), jnp.float32), 0.099609375, 1.8984375).astype(jnp.bfloat16)
    prompt_lengths = jax.vmap(lambda own: ragged(own, NPROMPT, G_TOK, MAXLEN, 2))(jax.random.split(key_list[4], GROUPS)).reshape((GROUPS, NPROMPT)).astype(jnp.int32)
    expert_ids_keys = jax.random.split(jax.random.fold_in(key_list[5], 1), TOKEN_TOTAL // TOK_DEV)
    expert_ids_turns = jax.random.permutation(jax.random.fold_in(key_list[5], 3), TOKEN_TOTAL // TOK_DEV)
    expert_ids = jax.vmap(lambda own, number: deal_out(jax.random.fold_in(key_list[5], 2), own, number, TOK_DEV, EXPERTS, TOPK, CAP, 2))(expert_ids_keys, expert_ids_turns).reshape((TOKEN_TOTAL, TOPK))
    router_logits = draw_router_logits(jax.random.fold_in(key_list[14], 71), 0)
    w_gate = scatter_about(key_list[7], (EXPERTS, D, FF), D ** -0.5, 0.125, ((0, 16),))
    w_up = scatter_about(key_list[8], (EXPERTS, D, FF), D ** -0.5, 0.125, ((0, 16),))
    w_down = scatter_about(key_list[9], (EXPERTS, FF, D), FF ** -0.5, 0.15625, ((0, 16),))
    w_shared_gate = scatter_about(key_list[10], (D, SFF), D ** -0.5, 0.125, ((0, 16), (1, 2)))
    w_shared_up = scatter_about(key_list[11], (D, SFF), D ** -0.5, 0.125, ((0, 16), (1, 2)))
    w_shared_down = scatter_about(key_list[12], (D, SFF), SFF ** -0.5, 0.109375, ((0, 16), (1, 2)))
    page_table = draw_page_table(jax.random.fold_in(key_list[14], 71), 0)
    return dict(queries=queries, keys_then_values=keys_then_values, residual=residual, norm_gain=norm_gain, prompt_lengths=prompt_lengths, expert_ids=expert_ids, router_logits=router_logits, w_gate=w_gate, w_up=w_up, w_down=w_down, w_shared_gate=w_shared_gate, w_shared_up=w_shared_up, w_shared_down=w_shared_down, page_table=page_table)


large_negative = -1e+30
eps_norm = 1e-06

def segment_ids(positions, prompt_ends):
    return lax.optimization_barrier(jnp.sum((positions[:, None] >= prompt_ends[None, :]).astype(jnp.int32), axis=1))

def group_attention(queries, keys_then_values, lengths):
    group_row_block = queries.shape[0]
    heads_per_group = QUERY_HEADS // KEY_VALUE_HEADS
    query_everything = queries.reshape(group_row_block, KEY_VALUE_HEADS, heads_per_group, HEAD_SIZE)
    key_row_block = keys_then_values[:, :KEY_VALUE_HEADS * HEAD_SIZE].reshape(group_row_block, KEY_VALUE_HEADS, HEAD_SIZE).astype(jnp.float32)
    value_row_block = keys_then_values[:, KEY_VALUE_HEADS * HEAD_SIZE:].reshape(group_row_block, KEY_VALUE_HEADS, HEAD_SIZE).astype(jnp.float32)
    prompt_ends = jnp.cumsum(lengths).astype(jnp.int32)
    key_pos = jnp.arange(group_row_block, dtype=jnp.int32)
    key_seg = segment_ids(key_pos, prompt_ends)
    block_rows = math.gcd(group_row_block, 512)

    def one_block(block_index):
        begin_at = (block_index * block_rows).astype(jnp.int32)
        query_block = lax.dynamic_slice_in_dim(query_everything, begin_at, block_rows, 0).astype(jnp.float32)
        query_pos = begin_at + jnp.arange(block_rows, dtype=jnp.int32)
        query_seg = segment_ids(query_pos, prompt_ends)
        scores = jnp.einsum('qhgd,khd->hgqk', query_block, key_row_block) * HEAD_SIZE ** (-0.5)
        visible = (key_pos[None, :] <= query_pos[:, None]) & (key_seg[None, :] == query_seg[:, None])
        scores = jnp.where(visible, scores, large_negative)
        row_max = lax.optimization_barrier(jnp.max(scores, axis=3, keepdims=True))
        exp_terms = jnp.where(visible, jnp.exp(scores - row_max), 0.0)
        row_total = lax.optimization_barrier(jnp.sum(exp_terms, axis=3))
        rounded = lax.optimization_barrier(exp_terms.astype(jnp.bfloat16)).astype(jnp.float32)
        mixed_heads = jnp.einsum('hgqk,khd->hgqd', rounded, value_row_block) / row_total[..., None]
        log_block = (row_max[..., 0] + jnp.log(row_total)).reshape(QUERY_HEADS, block_rows)
        return (jnp.transpose(mixed_heads, (2, 0, 1, 3)).reshape(block_rows, QUERY_HEADS * HEAD_SIZE).astype(jnp.bfloat16), log_block)
    blocks, log_blocks = lax.map(one_block, jnp.arange(group_row_block // block_rows, dtype=jnp.int32))
    log_group = jnp.transpose(log_blocks, (1, 0, 2)).reshape(QUERY_HEADS, group_row_block)
    return (blocks.reshape(group_row_block, QUERY_HEADS * HEAD_SIZE), log_group)

def reference(queries, keys_then_values, residual, norm_gain, prompt_lengths, expert_ids, router_logits, w_gate, w_up, w_down, w_shared_gate, w_shared_up, w_shared_down, page_table):
    group_row_block = TOK_DEV * N_EXP
    pieces_all = []
    log_pieces = []
    for group_index in range(GROUPS):
        lower = group_index * group_row_block
        upper = lower + group_row_block
        mixed_group, log_group = group_attention(queries[lower:upper], keys_then_values[lower:upper], prompt_lengths[group_index])
        pieces_all.append(mixed_group)
        log_pieces.append(log_group)
    attention = jnp.concatenate(pieces_all, axis=0)
    log_totals = jnp.concatenate(log_pieces, axis=1)
    hidden = residual.astype(jnp.float32) + attention.astype(jnp.float32)
    scale_rows = lax.rsqrt(lax.optimization_barrier(jnp.mean(hidden * hidden, axis=-1, keepdims=True)) + eps_norm)
    normed = (hidden * scale_rows * norm_gain.astype(jnp.float32)).astype(jnp.bfloat16)
    route_weights = jax.nn.softmax(router_logits.astype(jnp.float32), axis=-1)
    flat_ids = expert_ids.reshape(-1)
    flat_weights = jnp.concatenate([route_weights.reshape(-1), jnp.zeros((1,), jnp.float32)])
    normed_pad = jnp.concatenate([normed, jnp.zeros((1, D), jnp.bfloat16)], axis=0)
    most_rows = GROUPS * N_EXP * CAP

    def one_expert(mix_total, expert_index):
        pick_rows = jnp.nonzero(flat_ids == expert_index, size=most_rows, fill_value=TOKEN_TOTAL * TOPK)[0].astype(jnp.int32)
        token_index = pick_rows // TOPK
        inputs = normed_pad[token_index]
        gate_out = jnp.dot(inputs, w_gate[expert_index], preferred_element_type=jnp.float32)
        up_out = jnp.dot(inputs, w_up[expert_index], preferred_element_type=jnp.float32)
        activated = (jax.nn.silu(gate_out) * up_out).astype(jnp.bfloat16)
        expert_out = jnp.dot(activated, w_down[expert_index], preferred_element_type=jnp.float32).astype(jnp.bfloat16)
        mix_total = mix_total.at[token_index].add(flat_weights[pick_rows][:, None] * expert_out.astype(jnp.float32), mode='drop')
        return (mix_total, None)
    mix_total, _ = lax.scan(one_expert, jnp.zeros((TOKEN_TOTAL, D), jnp.float32), jnp.arange(EXPERTS, dtype=jnp.int32))
    shared_gate = jnp.dot(normed, w_shared_gate, preferred_element_type=jnp.float32)
    shared_up = jnp.dot(normed, w_shared_up, preferred_element_type=jnp.float32)
    shared_act = (jax.nn.silu(shared_gate) * shared_up).astype(jnp.bfloat16)
    shared_out = jnp.dot(shared_act, jnp.transpose(w_shared_down), preferred_element_type=jnp.float32).astype(jnp.bfloat16)
    layer_out = (hidden + mix_total + shared_out.astype(jnp.float32)).astype(jnp.bfloat16)
    key_value_width = 2 * KEY_VALUE_HEADS * HEAD_SIZE
    kv_pages = keys_then_values.reshape(GROUPS * GPAGES, PAGE, key_value_width)
    kv_cache = jnp.zeros((GROUPS * GPAGES, PAGE, key_value_width), jnp.bfloat16).at[page_table.reshape(-1)].set(kv_pages)
    return (layer_out, kv_cache, log_totals)
```

```python
import functools
import math

import jax
import jax.numpy as jnp
from jax import lax
from jax.experimental import pallas as pl
from jax.experimental.pallas import tpu as pltpu
from jax.sharding import PartitionSpec as P

D = 2048
QUERY_HEADS = 16
KEY_VALUE_HEADS = 4
HEAD_SIZE = 128
TOPK = 6
PAGE = 16
CORES = 2
Z_SIZE = 4

large_negative = -1e30
eps_norm = 1e-06
VMEM_LIMIT = 56 * 1024 * 1024
SCORE_SCALE = HEAD_SIZE ** (-0.5)
EXP2_SCALE = SCORE_SCALE * math.log2(math.e)


def attention_kernel(first, last, n_chunks, *refs):
    refs = list(refs)
    place_ref, lengths_ref = refs[0], refs[1]
    q_ref = refs[2]
    chunks = refs[3 : 3 + n_chunks]
    refs = refs[3 + n_chunks :]
    if not first:
        acc_in, max_in, sum_in = refs[:3]
        refs = refs[3:]
    if last:
        residual_ref, gain_ref = refs[:2]
        refs = refs[2:]
        hidden_out, normed_out, log_out, attn_scr = refs
    else:
        acc_out, max_out, sum_out = refs
    rows = q_ref.shape[0]
    heads = QUERY_HEADS // KEY_VALUE_HEADS
    key_rows = chunks[0].shape[0]
    query_pos = place_ref[0] + lax.broadcasted_iota(jnp.int32, (1, rows), 1)
    start = jnp.zeros((1, rows), jnp.int32)
    end = jnp.int32(0)
    for i in range(lengths_ref.shape[1]):
        end = end + lengths_ref[0, i]
        start = start + jnp.where(query_pos >= end, lengths_ref[0, i], 0)
    biases = []
    for j in range(n_chunks):
        key_pos = place_ref[1 + j] + lax.broadcasted_iota(jnp.int32, (key_rows, rows), 0)
        visible = (key_pos >= start) & (key_pos <= query_pos)
        biases.append(jnp.where(visible, 0.0, large_negative))
    bias = jnp.concatenate(biases, axis=0)
    bias = jnp.concatenate([bias] * heads, axis=1)
    for h in range(KEY_VALUE_HEADS):
        columns = slice(h * HEAD_SIZE, (h + 1) * HEAD_SIZE)
        value_columns = slice((KEY_VALUE_HEADS + h) * HEAD_SIZE, (KEY_VALUE_HEADS + h + 1) * HEAD_SIZE)
        keys = jnp.concatenate([c[:, columns] for c in chunks], axis=0)
        values = jnp.concatenate([c[:, value_columns] for c in chunks], axis=0)
        query = jnp.concatenate(
            [q_ref[:, (h * heads + g) * HEAD_SIZE : (h * heads + g + 1) * HEAD_SIZE] for g in range(heads)],
            axis=0,
        )
        scores = lax.dot_general(keys, query, (((1,), (1,)), ((), ())), preferred_element_type=jnp.float32)
        scores = scores + bias
        new_max = jnp.max(scores, axis=0, keepdims=True)
        if not first:
            old_max = max_in[h : h + 1, :]
            new_max = jnp.maximum(new_max, old_max)
            fade = jnp.exp2((old_max - new_max) * EXP2_SCALE)
        terms = jnp.exp2((scores - new_max) * EXP2_SCALE)
        total = jnp.sum(terms, axis=0, keepdims=True)
        mixed = lax.dot_general(
            values, terms.astype(jnp.bfloat16), (((0,), (0,)), ((), ())), preferred_element_type=jnp.float32
        )
        if not first:
            total = total + fade * sum_in[h : h + 1, :]
            mixed = mixed + fade * acc_in[h]
        if last:
            mixed = mixed / total
            log_row = new_max * SCORE_SCALE + jnp.log(total)
            for g in range(heads):
                part = mixed[:, g * rows : (g + 1) * rows]
                at = h * heads + g
                attn_scr[:, at * HEAD_SIZE : (at + 1) * HEAD_SIZE] = part.T
                log_out[at : at + 1, :] = log_row[:, g * rows : (g + 1) * rows]
        else:
            acc_out[h] = mixed
            max_out[h : h + 1, :] = new_max
            sum_out[h : h + 1, :] = total
    if last:
        attention = attn_scr[...].astype(jnp.bfloat16).astype(jnp.float32)
        hidden = residual_ref[...].astype(jnp.float32) + attention
        scale_rows = lax.rsqrt(jnp.mean(hidden * hidden, axis=-1, keepdims=True) + eps_norm)
        hidden_out[...] = hidden
        normed_out[...] = (hidden * scale_rows * gain_ref[...].astype(jnp.float32)).astype(jnp.bfloat16)


def attention_call(place, lengths, queries, chunks, state, finish):
    rows = queries.shape[0]
    heads = QUERY_HEADS // KEY_VALUE_HEADS
    first, last = state is None, finish is not None
    vmem, smem = pl.BlockSpec(memory_space=pltpu.VMEM), pl.BlockSpec(memory_space=pltpu.SMEM)
    operands = [place, lengths, queries, *chunks]
    if not first:
        operands += list(state)
    scratch = []
    if last:
        operands += list(finish)
        outs = [
            jax.ShapeDtypeStruct((rows, D), jnp.float32),
            jax.ShapeDtypeStruct((rows, D), jnp.bfloat16),
            jax.ShapeDtypeStruct((QUERY_HEADS, rows), jnp.float32),
        ]
        scratch = [pltpu.VMEM((rows, D), jnp.float32)]
    else:
        outs = [
            jax.ShapeDtypeStruct((KEY_VALUE_HEADS, HEAD_SIZE, heads * rows), jnp.float32),
            jax.ShapeDtypeStruct((KEY_VALUE_HEADS, heads * rows), jnp.float32),
            jax.ShapeDtypeStruct((KEY_VALUE_HEADS, heads * rows), jnp.float32),
        ]
    keys = sum(c.shape[0] for c in chunks)
    return pl.pallas_call(
        functools.partial(attention_kernel, first, last, len(chunks)),
        out_shape=outs,
        in_specs=[smem, smem] + [vmem] * (len(operands) - 2),
        out_specs=[vmem] * len(outs),
        scratch_shapes=scratch,
        compiler_params=pltpu.CompilerParams(vmem_limit_bytes=VMEM_LIMIT),
        cost_estimate=pl.CostEstimate(
            flops=4 * rows * keys * QUERY_HEADS * HEAD_SIZE,
            bytes_accessed=4 * rows * D * 3,
            transcendentals=rows * keys * QUERY_HEADS,
        ),
    )(*operands)


def pieces_of(width, step):
    return [(at, min(step, width - at)) for at in range(0, width, step)]


def experts_kernel(n_chunks, up_step, down_step, *refs):
    place_ref, share_ref = refs[0], refs[1]
    x_in = refs[2 : 2 + n_chunks]
    gate_in, up_in, down_in, shared_in = refs[2 + n_chunks : 6 + n_chunks]
    outs = refs[6 + n_chunks : 6 + 2 * n_chunks]
    x_scr, gate_scr, up_scr, down_scr, shared_scr, act_scr, sems = refs[6 + 2 * n_chunks :]
    rows = x_in[0].shape[0]
    hidden_units = gate_in.shape[2]
    shared_units = shared_in.shape[1]
    up_pieces, down_pieces = pieces_of(hidden_units, up_step), pieces_of(D, down_step)
    copies = []

    def start(source, target):
        copy = pltpu.make_async_copy(source, target, sems.at[len(copies)])
        copy.start()
        copies.append(copy)
        return copy

    x_copies = [start(x_in[j], x_scr.at[pl.ds(j * rows, rows)]) for j in range(n_chunks)]
    up_copies = [
        (
            start(gate_in.at[0, :, pl.ds(at, size)], gate_scr.at[:, pl.ds(at, size)]),
            start(up_in.at[0, :, pl.ds(at, size)], up_scr.at[:, pl.ds(at, size)]),
        )
        for at, size in up_pieces
    ]
    shared_copy = start(shared_in, shared_scr)
    down_copies = [
        start(down_in.at[0, :, pl.ds(at, size)], down_scr.at[:, pl.ds(at, size)]) for at, size in down_pieces
    ]
    expert = place_ref[0]
    scales = []
    for j in range(n_chunks):
        shares = share_ref[place_ref[1 + j]]
        lanes = lax.broadcasted_iota(jnp.int32, shares.shape, 1)
        scales.append(jnp.sum(jnp.where(lanes == expert, shares, 0.0), axis=1, keepdims=True))
    scale = jnp.concatenate(scales, axis=0)
    for copy in x_copies:
        copy.wait()
    for (at, size), (gate_copy, up_copy) in zip(up_pieces, up_copies):
        gate_copy.wait()
        gate = jnp.dot(x_scr[...], gate_scr[:, at : at + size], preferred_element_type=jnp.float32)
        up_copy.wait()
        up = jnp.dot(x_scr[...], up_scr[:, at : at + size], preferred_element_type=jnp.float32)
        act_scr[:, at : at + size] = (gate / (1.0 + jnp.exp(-gate)) * up * scale).astype(jnp.bfloat16)
    shared_copy.wait()
    across = (((1,), (1,)), ((), ()))
    gate = lax.dot_general(x_scr[...], shared_scr[0], across, preferred_element_type=jnp.float32)
    up = lax.dot_general(x_scr[...], shared_scr[1], across, preferred_element_type=jnp.float32)
    shared_act = (gate / (1.0 + jnp.exp(-gate)) * up).astype(jnp.bfloat16)
    for (at, size), copy in zip(down_pieces, down_copies):
        copy.wait()
        part = jnp.dot(act_scr[...], down_scr[:, at : at + size], preferred_element_type=jnp.float32)
        part = part + jnp.dot(shared_act, shared_scr[2, :, at : at + size], preferred_element_type=jnp.float32)
        part = part.astype(jnp.bfloat16)
        for j in range(n_chunks):
            outs[j][:, at : at + size] = part[j * rows : (j + 1) * rows, :]


def experts_call(place, shares, chunks, w_gate, w_up, w_down, shared):
    rows, n_chunks = chunks[0].shape[0], len(chunks)
    units, shared_units = w_gate.shape[2], shared.shape[1]
    up_step, down_step = 256, 512
    n_copies = n_chunks + 2 * len(pieces_of(units, up_step)) + 1 + len(pieces_of(D, down_step))
    vmem, smem = pl.BlockSpec(memory_space=pltpu.VMEM), pl.BlockSpec(memory_space=pltpu.SMEM)
    hbm = pl.BlockSpec(memory_space=pl.ANY)
    return pl.pallas_call(
        functools.partial(experts_kernel, n_chunks, up_step, down_step),
        out_shape=[jax.ShapeDtypeStruct((rows, D), jnp.bfloat16)] * n_chunks,
        in_specs=[smem, vmem] + [hbm] * (n_chunks + 4),
        out_specs=[vmem] * n_chunks,
        scratch_shapes=[
            pltpu.VMEM((n_chunks * rows, D), jnp.bfloat16),
            pltpu.VMEM((D, units), jnp.bfloat16),
            pltpu.VMEM((D, units), jnp.bfloat16),
            pltpu.VMEM((units, D), jnp.bfloat16),
            pltpu.VMEM((3, shared_units, D), jnp.bfloat16),
            pltpu.VMEM((n_chunks * rows, units), jnp.bfloat16),
            pltpu.SemaphoreType.DMA((n_copies,)),
        ],
        compiler_params=pltpu.CompilerParams(vmem_limit_bytes=VMEM_LIMIT),
        cost_estimate=pl.CostEstimate(
            flops=6 * n_chunks * rows * D * (units + shared_units),
            bytes_accessed=6 * D * (units + shared_units) + 4 * n_chunks * rows * D,
            transcendentals=n_chunks * rows * units,
        ),
    )(place, shares, *chunks, w_gate, w_up, w_down, shared)


def pages_kernel(n_groups, place_ref, table_ref, *refs):
    sources, out_ref = refs[:n_groups], refs[n_groups]
    pages_dev = out_ref.shape[0]
    for i in range(n_groups):
        for j in range(pages_dev):
            slot = table_ref[place_ref[2 + i], place_ref[0] + j] - place_ref[1]

            @pl.when((slot >= 0) & (slot < pages_dev))
            def _():
                out_ref[slot] = sources[i][j]


def pages_call(place, table, sources):
    vmem, smem = pl.BlockSpec(memory_space=pltpu.VMEM), pl.BlockSpec(memory_space=pltpu.SMEM)
    return pl.pallas_call(
        functools.partial(pages_kernel, len(sources)),
        out_shape=jax.ShapeDtypeStruct(sources[0].shape, jnp.bfloat16),
        in_specs=[smem, smem] + [vmem] * len(sources),
        out_specs=vmem,
        compiler_params=pltpu.CompilerParams(vmem_limit_bytes=VMEM_LIMIT),
    )(place, table, *sources)


def on_device(
    queries,
    keys_then_values,
    residual,
    norm_gain,
    prompt_lengths,
    expert_ids,
    router_logits,
    w_gate,
    w_up,
    w_down,
    w_shared_gate,
    w_shared_up,
    w_shared_down,
    page_table,
):
    token_rows = queries.shape[0]
    n_groups = lax.axis_size("req")
    n_columns = lax.axis_size("exp")
    column = lax.axis_index("exp")
    my_group = lax.axis_index("req")
    n_z, n_x = Z_SIZE, n_columns // (Z_SIZE * CORES)
    my_z, my_x, my_c = column // (n_x * CORES), (column // CORES) % n_x, column % CORES

    def place_of(z, x, c):
        return (z * n_x + x) * CORES + c

    def moved(dz, dx, dc):
        return [
            (place_of(z, x, c), place_of((z + dz) % n_z, (x + dx) % n_x, (c + dc) % CORES))
            for z in range(n_z)
            for x in range(n_x)
            for c in range(CORES)
        ]

    def hop(value, dz=0, dx=0, dc=0):
        return lax.ppermute(value, "exp", moved(dz, dx, dc))

    def gather_steps(own):
        steps = []
        held = own
        for s in range(n_z):
            if s > 0:
                held = hop(held, dz=1)
            across = [held] + [hop(held, dx=i) for i in range(1, n_x)]
            steps.append(across + [hop(a, dc=1) for a in across])
        return steps

    def sources_of(s):
        return [
            place_of((my_z - s) % n_z, (my_x - i) % n_x, (my_c + j) % CORES)
            for j in range(CORES)
            for i in range(n_x)
        ]

    shared = jnp.stack([w.T for w in (w_shared_gate, w_shared_up, w_shared_down)])
    units = shared.shape[1] // n_columns
    shared = shared.reshape(3, n_columns, units, token_rows_of(w_shared_gate)).transpose(1, 0, 2, 3)
    shared = lax.all_to_all(shared, "exp", split_axis=0, concat_axis=0, tiled=True)
    halves = [shared] + [
        lax.ppermute(shared, "req", [(g, (g + i) % n_groups) for g in range(n_groups)]) for i in range(1, n_groups)
    ]
    shared = jnp.stack(halves).transpose(2, 0, 3, 1, 4).reshape(3, n_groups * units, D)

    weights = jax.nn.softmax(router_logits, axis=-1)
    experts = w_gate.shape[0] * n_columns
    chosen = expert_ids[:, :, None] == jnp.arange(experts, dtype=jnp.int32)[None, None, :]
    shares = jnp.sum(jnp.where(chosen, weights[:, :, None], 0.0), axis=1)
    shares = lax.all_gather(shares, "exp", axis=0, tiled=False)

    kv_steps = gather_steps(keys_then_values)
    own_place = column * token_rows
    state = None
    for s, chunks in enumerate(kv_steps):
        place = jnp.stack([own_place] + [a * token_rows for a in sources_of(s)]).astype(jnp.int32)
        finish = (residual, norm_gain.reshape(1, D)) if s == n_z - 1 else None
        state = attention_call(place, prompt_lengths, queries, chunks, state, finish)
    hidden, normed, log_totals = state

    pages_dev = token_rows // PAGE
    own_pages = keys_then_values.reshape(pages_dev, PAGE, keys_then_values.shape[1])
    page_sources = [own_pages] + [
        lax.ppermute(own_pages, "req", [(g, (g + i) % n_groups) for g in range(n_groups)]) for i in range(1, n_groups)
    ]
    group_pages = pages_dev * n_columns
    place = jnp.stack(
        [column * pages_dev, my_group * group_pages + column * pages_dev]
        + [(my_group - i) % n_groups for i in range(n_groups)]
    ).astype(jnp.int32)
    kv_cache = pages_call(place, page_table, page_sources)

    row_steps = gather_steps(normed)
    partial = []
    for s, chunks in enumerate(row_steps):
        place = jnp.stack([column] + sources_of(s)).astype(jnp.int32)
        outs = experts_call(place, shares, chunks, w_gate, w_up, w_down, shared)
        from_core = [hop(a, dc=1) for a in outs[n_x:]]
        ours = outs[:n_x]
        across = [
            hop((ours[i].astype(jnp.float32) + from_core[i].astype(jnp.float32)).astype(jnp.bfloat16), dx=-i)
            for i in range(1, n_x)
        ]
        partial.append([ours[0], from_core[0]] + across)

    def summed(parts):
        total = parts[0].astype(jnp.float32)
        for part in parts[1:]:
            total = total + part.astype(jnp.float32)
        return total

    ring = None
    for s in list(range(1, n_z)) + [0]:
        parts = partial[s] if ring is None else partial[s] + [hop(ring, dz=1)]
        if s != 0:
            ring = summed(parts).astype(jnp.bfloat16)
        else:
            layer_out = (hidden + summed(parts)).astype(jnp.bfloat16)
    return (layer_out, kv_cache, log_totals)


def token_rows_of(weight):
    return weight.shape[0]


def solution(mesh):
    placed = (
        P(("req", "exp"), None),
        P(("req", "exp"), None),
        P(("req", "exp"), None),
        P(),
        P("req", None),
        P(("req", "exp"), None),
        P(("req", "exp"), None),
        P("exp", None, None),
        P("exp", None, None),
        P("exp", None, None),
        P("exp", "req"),
        P("exp", "req"),
        P("exp", "req"),
        P(),
    )
    return jax.shard_map(
        on_device,
        mesh=mesh,
        in_specs=placed,
        out_specs=(P(("req", "exp"), None), P(("req", "exp"), None, None), P(None, ("req", "exp"))),
        check_vma=False,
    )
```

```python
import functools
import math

import jax
import jax.numpy as jnp
from jax import lax
from jax.experimental import pallas as pl
from jax.experimental.pallas import tpu as pltpu
from jax.sharding import PartitionSpec as P

D = 2048
QUERY_HEADS = 16
KEY_VALUE_HEADS = 4
HEAD_SIZE = 128
TOPK = 6
PAGE = 16
CORES = 2
Z_SIZE = 4

large_negative = -1e30
eps_norm = 1e-06
VMEM_LIMIT = 56 * 1024 * 1024
SCORE_SCALE = HEAD_SIZE ** (-0.5)
EXP2_SCALE = SCORE_SCALE * math.log2(math.e)


def attention_kernel(first, last, n_blocks, *refs):
    refs = list(refs)
    place_ref, lengths_ref = refs[:2]
    queries = refs[2 : 2 + CORES]
    blocks = refs[2 + CORES : 2 + CORES + n_blocks]
    refs = refs[2 + CORES + n_blocks :]
    if not first:
        acc_in, max_in, sum_in = refs[:3]
        refs = refs[3:]
    rows = queries[0].shape[0]
    kv_heads = KEY_VALUE_HEADS // CORES
    heads = QUERY_HEADS // KEY_VALUE_HEADS
    wide = CORES * rows
    iota = lax.broadcasted_iota(jnp.int32, (1, rows), 1)
    query_pos = jnp.concatenate([place_ref[i] + iota for i in range(CORES)], axis=1)
    start = jnp.zeros((1, wide), jnp.int32)
    end = jnp.int32(0)
    for i in range(lengths_ref.shape[1]):
        end = end + lengths_ref[0, i]
        start = start + jnp.where(query_pos >= end, lengths_ref[0, i], 0)
    biases = []
    for j in range(n_blocks * CORES):
        key_pos = place_ref[CORES + j] + lax.broadcasted_iota(jnp.int32, (rows, wide), 0)
        visible = (key_pos >= start) & (key_pos <= query_pos)
        biases.append(jnp.where(visible, 0.0, large_negative))
    bias = jnp.concatenate(biases, axis=0)
    bias = jnp.concatenate([bias] * heads, axis=1)
    for h in range(kv_heads):
        columns = slice(h * HEAD_SIZE, (h + 1) * HEAD_SIZE)
        value_columns = slice((kv_heads + h) * HEAD_SIZE, (kv_heads + h + 1) * HEAD_SIZE)
        keys = jnp.concatenate([b[:, columns] for b in blocks], axis=0)
        values = jnp.concatenate([b[:, value_columns] for b in blocks], axis=0)
        query = jnp.concatenate(
            [
                q[:, (h * heads + g) * HEAD_SIZE : (h * heads + g + 1) * HEAD_SIZE]
                for g in range(heads)
                for q in queries
            ],
            axis=0,
        )
        scores = lax.dot_general(keys, query, (((1,), (1,)), ((), ())), preferred_element_type=jnp.float32)
        scores = scores + bias
        new_max = jnp.max(scores, axis=0, keepdims=True)
        if not first:
            old_max = max_in[h : h + 1, :]
            new_max = jnp.maximum(new_max, old_max)
            fade = jnp.exp2((old_max - new_max) * EXP2_SCALE)
        terms = jnp.exp2((scores - new_max) * EXP2_SCALE)
        total = jnp.sum(terms, axis=0, keepdims=True)
        mixed = lax.dot_general(
            values, terms.astype(jnp.bfloat16), (((0,), (0,)), ((), ())), preferred_element_type=jnp.float32
        )
        if not first:
            total = total + fade * sum_in[h : h + 1, :]
            mixed = mixed + fade * acc_in[h]
        if last:
            mixed = mixed / total
            log_row = new_max * SCORE_SCALE + jnp.log(total)
            for g in range(heads):
                for i in range(CORES):
                    part = slice(g * wide + i * rows, g * wide + (i + 1) * rows)
                    at = h * heads + g
                    refs[i][:, at * HEAD_SIZE : (at + 1) * HEAD_SIZE] = mixed[:, part].T.astype(jnp.bfloat16)
                    refs[CORES + i][at : at + 1, :] = log_row[:, part]
        else:
            refs[0][h] = mixed
            refs[1][h : h + 1, :] = new_max
            refs[2][h : h + 1, :] = total


def attention_call(place, lengths, queries, blocks, state, last):
    rows, columns = queries[0].shape
    kv_heads = KEY_VALUE_HEADS // CORES
    wide = CORES * rows * (QUERY_HEADS // KEY_VALUE_HEADS)
    vmem, smem = pl.BlockSpec(memory_space=pltpu.VMEM), pl.BlockSpec(memory_space=pltpu.SMEM)
    operands = [place, lengths, *queries, *blocks] + ([] if state is None else list(state))
    if last:
        outs = [jax.ShapeDtypeStruct((rows, columns), jnp.bfloat16)] * CORES
        outs += [jax.ShapeDtypeStruct((QUERY_HEADS // CORES, rows), jnp.float32)] * CORES
    else:
        outs = [jax.ShapeDtypeStruct((kv_heads, HEAD_SIZE, wide), jnp.float32)]
        outs += [jax.ShapeDtypeStruct((kv_heads, wide), jnp.float32)] * 2
    keys = sum(b.shape[0] for b in blocks)
    return pl.pallas_call(
        functools.partial(attention_kernel, state is None, last, len(blocks)),
        out_shape=outs,
        in_specs=[smem, smem] + [vmem] * (len(operands) - 2),
        out_specs=[vmem] * len(outs),
        compiler_params=pltpu.CompilerParams(vmem_limit_bytes=VMEM_LIMIT),
        cost_estimate=pl.CostEstimate(
            flops=4 * rows * keys * QUERY_HEADS * HEAD_SIZE,
            bytes_accessed=4 * rows * D * 3,
            transcendentals=rows * keys * QUERY_HEADS,
        ),
    )(*operands)


def norm_kernel(place_ref, mine_ref, other_ref, residual_ref, gain_ref, hidden_out, normed_out):
    width = mine_ref.shape[1]
    squares = 0.0
    spans = [pl.ds(pl.multiple_of(place_ref[i] * width, width), width) for i in range(CORES)]
    for span, part in zip(spans, (mine_ref, other_ref)):
        hidden = residual_ref[:, span].astype(jnp.float32) + part[...].astype(jnp.float32)
        hidden_out[:, span] = hidden
        squares = squares + jnp.sum(hidden * hidden, axis=-1, keepdims=True)
    scale_rows = lax.rsqrt(squares / residual_ref.shape[1] + eps_norm)
    normed_out[...] = (hidden_out[...] * scale_rows * gain_ref[...].astype(jnp.float32)).astype(jnp.bfloat16)


def norm_call(place, mine, other, residual, gain):
    vmem, smem = pl.BlockSpec(memory_space=pltpu.VMEM), pl.BlockSpec(memory_space=pltpu.SMEM)
    return pl.pallas_call(
        norm_kernel,
        out_shape=[
            jax.ShapeDtypeStruct(residual.shape, jnp.float32),
            jax.ShapeDtypeStruct(residual.shape, jnp.bfloat16),
        ],
        in_specs=[smem] + [vmem] * 4,
        out_specs=[vmem] * 2,
        compiler_params=pltpu.CompilerParams(vmem_limit_bytes=VMEM_LIMIT),
    )(place, mine, other, residual, gain)


def pieces_of(width, step):
    return [(at, min(step, width - at)) for at in range(0, width, step)]


def silu(value):
    return value / (1.0 + jnp.exp(-value))


def experts_kernel(n_blocks, up_step, down_step, ahead, *refs):
    place_ref, share_ref = refs[0], refs[1]
    x_in = refs[2 : 2 + n_blocks]
    refs = refs[2 + n_blocks :]
    experts = [refs[3 * e : 3 * e + 3] for e in range(CORES)]
    shared_in = refs[3 * CORES]
    refs = refs[3 * CORES + 1 :]
    outs = refs[:n_blocks]
    refs = refs[n_blocks:]
    x_scr, shared_scr, act_scr, sems = refs[:4]
    held = [refs[4 + 3 * e : 7 + 3 * e] for e in range(CORES)]
    rows = x_in[0].shape[0]
    units = act_scr.shape[2]
    up_pieces, down_pieces = pieces_of(units, up_step), pieces_of(D, down_step)
    groups, taken = [], 0

    def group(*pairs):
        nonlocal taken
        groups.append([pltpu.make_async_copy(a, b, sems.at[taken + i]) for i, (a, b) in enumerate(pairs)])
        taken += len(pairs)

    for e in range(CORES):
        for at, size in up_pieces:
            span = pl.ds(at, size)
            group(*[(experts[e][i].at[0, :, span], held[e][i].at[:, span]) for i in range(2)])
    group((shared_in, shared_scr))
    for at, size in down_pieces:
        span = pl.ds(at, size)
        group(*[(experts[e][2].at[0, :, span], held[e][2].at[:, span]) for e in range(CORES)])

    def start(i):
        if i < len(groups):
            for copy in groups[i]:
                copy.start()

    turn = 0

    def arrived():
        nonlocal turn
        start(turn + ahead)
        for copy in groups[turn]:
            copy.wait()
        turn += 1

    x_copies = [
        pltpu.make_async_copy(x_in[j], x_scr.at[pl.ds(j * rows, rows)], sems.at[taken + j]) for j in range(n_blocks)
    ]
    for copy in x_copies:
        copy.start()
    for i in range(ahead):
        start(i)
    scales = []
    for e in range(CORES):
        columns = []
        for j in range(n_blocks):
            shares = share_ref[place_ref[CORES + j]]
            lanes = lax.broadcasted_iota(jnp.int32, shares.shape, 1)
            columns.append(jnp.sum(jnp.where(lanes == place_ref[e], shares, 0.0), axis=1, keepdims=True))
        scales.append(jnp.concatenate(columns, axis=0))
    for copy in x_copies:
        copy.wait()
    x = x_scr[...]
    for e in range(CORES):
        for at, size in up_pieces:
            arrived()
            gate = jnp.dot(x, held[e][0][:, at : at + size], preferred_element_type=jnp.float32)
            up = jnp.dot(x, held[e][1][:, at : at + size], preferred_element_type=jnp.float32)
            act_scr[e, :, at : at + size] = (silu(gate) * up * scales[e]).astype(jnp.bfloat16)
    arrived()
    across = (((1,), (1,)), ((), ()))
    gate = lax.dot_general(x, shared_scr[0], across, preferred_element_type=jnp.float32)
    up = lax.dot_general(x, shared_scr[1], across, preferred_element_type=jnp.float32)
    shared_act = (silu(gate) * up).astype(jnp.bfloat16)
    for at, size in down_pieces:
        arrived()
        part = jnp.dot(shared_act, shared_scr[2, :, at : at + size], preferred_element_type=jnp.float32)
        for e in range(CORES):
            part = part + jnp.dot(act_scr[e], held[e][2][:, at : at + size], preferred_element_type=jnp.float32)
        part = part.astype(jnp.bfloat16)
        for j in range(n_blocks):
            outs[j][:, at : at + size] = part[j * rows : (j + 1) * rows, :]


def experts_call(place, shares, blocks, weights, shared):
    rows, n_blocks = blocks[0].shape[0], len(blocks)
    units, shared_units = weights[0].shape[2], shared.shape[1]
    up_step, down_step, ahead = 256, 512, 4
    n_copies = n_blocks + CORES * (2 * len(pieces_of(units, up_step)) + len(pieces_of(D, down_step))) + 1
    vmem, smem = pl.BlockSpec(memory_space=pltpu.VMEM), pl.BlockSpec(memory_space=pltpu.SMEM)
    hbm = pl.BlockSpec(memory_space=pl.ANY)
    held = [
        pltpu.VMEM((D, units), jnp.bfloat16),
        pltpu.VMEM((D, units), jnp.bfloat16),
        pltpu.VMEM((units, D), jnp.bfloat16),
    ]
    return pl.pallas_call(
        functools.partial(experts_kernel, n_blocks, up_step, down_step, ahead),
        out_shape=[jax.ShapeDtypeStruct((rows, D), jnp.bfloat16)] * n_blocks,
        in_specs=[smem, vmem] + [hbm] * (n_blocks + len(weights) + 1),
        out_specs=[vmem] * n_blocks,
        scratch_shapes=[
            pltpu.VMEM((n_blocks * rows, D), jnp.bfloat16),
            pltpu.VMEM((3, shared_units, D), jnp.bfloat16),
            pltpu.VMEM((CORES, n_blocks * rows, units), jnp.bfloat16),
            pltpu.SemaphoreType.DMA((n_copies,)),
        ]
        + held * CORES,
        compiler_params=pltpu.CompilerParams(vmem_limit_bytes=VMEM_LIMIT),
        cost_estimate=pl.CostEstimate(
            flops=6 * n_blocks * rows * D * (CORES * units + shared_units),
            bytes_accessed=6 * D * (CORES * units + shared_units) + 4 * n_blocks * rows * D,
            transcendentals=n_blocks * rows * units,
        ),
    )(place, shares, *blocks, *weights, shared)


def pages_kernel(n_groups, place_ref, table_ref, *refs):
    sources, out_ref = refs[:n_groups], refs[n_groups]
    pages_dev = out_ref.shape[0]
    for i in range(n_groups):
        for j in range(pages_dev):
            slot = table_ref[place_ref[2 + i], place_ref[0] + j] - place_ref[1]

            @pl.when((slot >= 0) & (slot < pages_dev))
            def _():
                out_ref[slot] = sources[i][j]


def pages_call(place, table, sources):
    vmem, smem = pl.BlockSpec(memory_space=pltpu.VMEM), pl.BlockSpec(memory_space=pltpu.SMEM)
    return pl.pallas_call(
        functools.partial(pages_kernel, len(sources)),
        out_shape=jax.ShapeDtypeStruct(sources[0].shape, jnp.bfloat16),
        in_specs=[smem, smem] + [vmem] * len(sources),
        out_specs=vmem,
        compiler_params=pltpu.CompilerParams(vmem_limit_bytes=VMEM_LIMIT),
    )(place, table, *sources)


def on_device(
    queries,
    keys_then_values,
    residual,
    norm_gain,
    prompt_lengths,
    expert_ids,
    router_logits,
    w_gate,
    w_up,
    w_down,
    w_shared_gate,
    w_shared_up,
    w_shared_down,
    page_table,
):
    token_rows = queries.shape[0]
    n_groups = lax.axis_size("req")
    n_columns = lax.axis_size("exp")
    column = lax.axis_index("exp")
    my_group = lax.axis_index("req")
    n_z, n_x = Z_SIZE, n_columns // (Z_SIZE * CORES)
    my_z, my_x, my_c = column // (n_x * CORES), (column // CORES) % n_x, column % CORES
    after = lax.optimization_barrier

    def place_of(z, x, c):
        return (z * n_x + x) * CORES + c

    def moved(dz, dx, dc):
        return [
            (place_of(z, x, c), place_of((z + dz) % n_z, (x + dx) % n_x, (c + dc) % CORES))
            for z in range(n_z)
            for x in range(n_x)
            for c in range(CORES)
        ]

    def hop(value, dz=0, dx=0, dc=0):
        return lax.ppermute(value, "exp", moved(dz, dx, dc))

    def hop_group(value, i):
        return lax.ppermute(value, "req", [(g, (g + i) % n_groups) for g in range(n_groups)])

    def gather_steps(own):
        steps = []
        held = own
        for s in range(n_z):
            if s > 0:
                held = hop(held, dz=1)
            steps.append([held] + [hop(held, dx=i) for i in range(1, n_x)])
        return steps

    def sources_of(s, parity):
        return [place_of((my_z - s) % n_z, (my_x - i) % n_x, (my_c + parity) % CORES) for i in range(n_x)]

    def numbers(values):
        return jnp.stack([jnp.asarray(v, jnp.int32) for v in values])

    width = D // CORES
    kv_width = KEY_VALUE_HEADS // CORES * HEAD_SIZE
    kv_pair = keys_then_values.reshape(token_rows, 2, KEY_VALUE_HEADS * HEAD_SIZE)
    kv_mine, kv_other = [
        lax.dynamic_slice_in_dim(kv_pair, c * kv_width, kv_width, 2).reshape(token_rows, 2 * kv_width)
        for c in (my_c, 1 - my_c)
    ]
    q_mine, q_other = [lax.dynamic_slice_in_dim(queries, c * width, width, 1) for c in (my_c, 1 - my_c)]
    kv_chip = jnp.concatenate([kv_mine, hop(kv_other, dc=1)], axis=0)
    q_chip = [q_mine, hop(q_other, dc=1)]
    kv_steps = gather_steps(kv_chip)

    own_weights, _ = after(((w_gate, w_up, w_down), kv_chip))
    weights = list(own_weights) + [hop(w, dc=1) for w in own_weights]

    route = jax.nn.softmax(router_logits, axis=-1)
    lanes = 128
    chosen = expert_ids[:, :, None] == jnp.arange(lanes, dtype=jnp.int32)[None, None, :]
    shares = jnp.sum(jnp.where(chosen, route[:, :, None], 0.0), axis=1)
    shares = lax.all_gather(shares, "exp", axis=0, tiled=False)

    own_shared, _ = after(((w_shared_gate, w_shared_up, w_shared_down), kv_steps[1][0]))
    feature_rows = w_shared_gate.shape[0]
    shared = jnp.stack([w.T for w in own_shared])
    units = shared.shape[1] // n_columns
    shared = shared.reshape(3, n_columns, units, feature_rows).transpose(1, 0, 2, 3)
    shared, _ = after((shared, kv_steps[-1][-1]))
    shared = lax.all_to_all(shared, "exp", split_axis=0, concat_axis=0, tiled=True)
    shared = jnp.stack([shared] + [hop_group(shared, i) for i in range(1, n_groups)])
    shared = shared.transpose(2, 0, 3, 1, 4).reshape(3, n_groups * units, D)
    shared = jnp.concatenate([shared, hop(shared, dc=1)], axis=1)

    own_places = [place_of(my_z, my_x, (my_c + i) % CORES) for i in range(CORES)]
    state = None
    for s, blocks in enumerate(kv_steps):
        keys_at = [a for pair in zip(*[sources_of(s, i) for i in range(CORES)]) for a in pair]
        place = numbers([a * token_rows for a in own_places + keys_at])
        state = attention_call(place, prompt_lengths, q_chip, blocks, state, s == n_z - 1)
    attn_mine, attn_other, log_mine, log_other = state
    attn_got, log_got = hop(attn_other, dc=1), hop(log_other, dc=1)
    hidden, normed = norm_call(numbers([my_c, 1 - my_c]), attn_mine, attn_got, residual, norm_gain.reshape(1, D))
    log_totals = jnp.where(
        my_c == 0, jnp.concatenate([log_mine, log_got], axis=0), jnp.concatenate([log_got, log_mine], axis=0)
    )

    pages_dev = token_rows // PAGE
    own_pages = keys_then_values.reshape(pages_dev, PAGE, keys_then_values.shape[1])
    own_pages, _ = after((own_pages, kv_steps[-1][-1]))
    page_sources = [own_pages] + [hop_group(own_pages, i) for i in range(1, n_groups)]
    group_pages = pages_dev * n_columns
    place = numbers(
        [column * pages_dev, my_group * group_pages + column * pages_dev]
        + [(my_group - i) % n_groups for i in range(n_groups)]
    )
    kv_cache = pages_call(place, page_table, page_sources)

    row_steps = gather_steps(normed)
    partial = []
    for s, blocks in enumerate(row_steps):
        place = numbers(own_places + sources_of(s, 0))
        if s == 0:
            place, kv_cache = after((place, kv_cache))
        outs = experts_call(place, shares, blocks, weights, shared)
        if s == 0:
            outs, _ = after((outs, row_steps[-1][-1]))
        partial.append([outs[0]] + [hop(outs[i], dx=-i) for i in range(1, n_x)])

    def summed(parts):
        total = parts[0].astype(jnp.float32)
        for part in parts[1:]:
            total = total + part.astype(jnp.float32)
        return total

    ring = None
    for s in list(range(1, n_z)) + [0]:
        parts = partial[s] if ring is None else partial[s] + [hop(ring, dz=1)]
        if s != 0:
            ring = summed(parts).astype(jnp.bfloat16)
        else:
            layer_out = (hidden + summed(parts)).astype(jnp.bfloat16)
    return (layer_out, kv_cache, log_totals)


def solution(mesh):
    placed = (
        P(("req", "exp"), None),
        P(("req", "exp"), None),
        P(("req", "exp"), None),
        P(),
        P("req", None),
        P(("req", "exp"), None),
        P(("req", "exp"), None),
        P("exp", None, None),
        P("exp", None, None),
        P("exp", None, None),
        P("exp", "req"),
        P("exp", "req"),
        P("exp", "req"),
        P(),
    )
    return jax.shard_map(
        on_device,
        mesh=mesh,
        in_specs=placed,
        out_specs=(P(("req", "exp"), None), P(("req", "exp"), None, None), P(None, ("req", "exp"))),
        check_vma=False,
    )
```

```python
import functools
import math

import jax
import jax.numpy as jnp
from jax import lax
from jax.experimental import pallas as pl
from jax.experimental.pallas import tpu as pltpu
from jax.sharding import PartitionSpec as P

D = 2048
QUERY_HEADS = 16
KEY_VALUE_HEADS = 4
HEAD_SIZE = 128
TOPK = 6
PAGE = 16
CORES = 2
Z_SIZE = 4

large_negative = -1e30
eps_norm = 1e-06
SMALL_LIMIT = 14 * 1024 * 1024
EXPERT_LIMIT = 8 * 1024 * 1024
ASSEMBLE_LIMIT = 2 * 1024 * 1024
HOLD_LIMIT = 16 * 1024 * 1024
LANES = 128
HALF_LANES = 64
SMALL_COST = pl.CostEstimate(flops=1000, bytes_accessed=1000, transcendentals=0)
SCORE_SCALE = HEAD_SIZE ** (-0.5)
EXP2_SCALE = SCORE_SCALE * math.log2(math.e)


def place_of(n_x, z, x, c):
    return (z * n_x + x) * CORES + c


def source_of(where_ref, n_z, n_x, s, i, parity):
    z = lax.rem(where_ref[1] + n_z - s, n_z)
    x = lax.rem(where_ref[2] + n_x - i, n_x)
    return place_of(n_x, z, x, lax.rem(where_ref[3] + parity, CORES))


def attention_kernel(first, last, n_z, n_x, s, *refs):
    refs = list(refs)
    where_ref, lengths_ref = refs[:2]
    n_blocks = n_x
    queries = refs[2 : 2 + CORES]
    blocks = refs[2 + CORES : 2 + CORES + n_blocks]
    refs = refs[2 + CORES + n_blocks :]
    if not first:
        acc_in, max_in, sum_in = refs[:3]
        refs = refs[3:]
    rows = queries[0].shape[0]
    kv_heads = KEY_VALUE_HEADS // CORES
    heads = QUERY_HEADS // KEY_VALUE_HEADS
    wide = CORES * rows
    iota = lax.broadcasted_iota(jnp.int32, (1, rows), 1)
    query_pos = jnp.concatenate(
        [source_of(where_ref, n_z, n_x, 0, 0, i) * rows + iota for i in range(CORES)], axis=1
    )
    start = jnp.zeros((1, wide), jnp.int32)
    end = jnp.int32(0)
    for i in range(lengths_ref.shape[1]):
        end = end + lengths_ref[0, i]
        start = start + jnp.where(query_pos >= end, lengths_ref[0, i], 0)
    biases = []
    for j in range(n_blocks * CORES):
        key_pos = source_of(where_ref, n_z, n_x, s, j // CORES, j % CORES) * rows
        key_pos = key_pos + lax.broadcasted_iota(jnp.int32, (rows, wide), 0)
        visible = (key_pos >= start) & (key_pos <= query_pos)
        biases.append(jnp.where(visible, 0.0, large_negative))
    bias = jnp.concatenate(biases, axis=0)
    bias = jnp.concatenate([bias] * heads, axis=1)
    for h in range(kv_heads):
        columns = slice(h * HEAD_SIZE, (h + 1) * HEAD_SIZE)
        value_columns = slice((kv_heads + h) * HEAD_SIZE, (kv_heads + h + 1) * HEAD_SIZE)
        keys = jnp.concatenate([b[:, columns] for b in blocks], axis=0)
        values = jnp.concatenate([b[:, value_columns] for b in blocks], axis=0)
        query = jnp.concatenate(
            [
                q[:, (h * heads + g) * HEAD_SIZE : (h * heads + g + 1) * HEAD_SIZE]
                for g in range(heads)
                for q in queries
            ],
            axis=0,
        )
        scores = lax.dot_general(keys, query, (((1,), (1,)), ((), ())), preferred_element_type=jnp.float32)
        scores = scores + bias
        new_max = jnp.max(scores, axis=0, keepdims=True)
        if not first:
            old_max = max_in[h : h + 1, :]
            new_max = jnp.maximum(new_max, old_max)
            fade = jnp.exp2((old_max - new_max) * EXP2_SCALE)
        terms = jnp.exp2((scores - new_max) * EXP2_SCALE)
        total = jnp.sum(terms, axis=0, keepdims=True)
        mixed = lax.dot_general(
            values, terms.astype(jnp.bfloat16), (((0,), (0,)), ((), ())), preferred_element_type=jnp.float32
        )
        if not first:
            total = total + fade * sum_in[h : h + 1, :]
            mixed = mixed + fade * acc_in[h]
        if last:
            mixed = mixed / total
            log_row = new_max * SCORE_SCALE + jnp.log(total)
            for g in range(heads):
                for i in range(CORES):
                    part = slice(g * wide + i * rows, g * wide + (i + 1) * rows)
                    at = h * heads + g
                    refs[i][:, at * HEAD_SIZE : (at + 1) * HEAD_SIZE] = mixed[:, part].T.astype(jnp.bfloat16)
                    refs[CORES + i][at : at + 1, :] = log_row[:, part]
        else:
            refs[0][h] = mixed
            refs[1][h : h + 1, :] = new_max
            refs[2][h : h + 1, :] = total


def attention_call(where, n_z, s, lengths, queries, blocks, state):
    rows, columns = queries[0].shape
    last = s == n_z - 1
    kv_heads = KEY_VALUE_HEADS // CORES
    wide = CORES * rows * (QUERY_HEADS // KEY_VALUE_HEADS)
    vmem, smem = pl.BlockSpec(memory_space=pltpu.VMEM), pl.BlockSpec(memory_space=pltpu.SMEM)
    operands = [where, lengths, *queries, *blocks] + ([] if state is None else list(state))
    if last:
        outs = [jax.ShapeDtypeStruct((rows, columns), jnp.bfloat16)] * CORES
        outs += [jax.ShapeDtypeStruct((QUERY_HEADS // CORES, rows), jnp.float32)] * CORES
    else:
        outs = [jax.ShapeDtypeStruct((kv_heads, HEAD_SIZE, wide), jnp.float32)]
        outs += [jax.ShapeDtypeStruct((kv_heads, wide), jnp.float32)] * 2
    keys = sum(b.shape[0] for b in blocks)
    return pl.pallas_call(
        functools.partial(attention_kernel, state is None, last, n_z, len(blocks), s),
        out_shape=outs,
        in_specs=[smem, smem] + [vmem] * (len(operands) - 2),
        out_specs=[vmem] * len(outs),
        compiler_params=pltpu.CompilerParams(vmem_limit_bytes=SMALL_LIMIT),
        cost_estimate=SMALL_COST,
    )(*operands)


def norm_kernel(where_ref, mine_ref, other_ref, residual_ref, gain_ref, ids_ref, logits_ref, hidden_out, rows_out):
    width = mine_ref.shape[1]
    squares = 0.0
    for i, part in enumerate((mine_ref, other_ref)):
        span = pl.ds(pl.multiple_of(lax.rem(where_ref[3] + i, CORES) * width, width), width)
        hidden = residual_ref[:, span].astype(jnp.float32) + part[...].astype(jnp.float32)
        hidden_out[:, span] = hidden
        squares = squares + jnp.sum(hidden * hidden, axis=-1, keepdims=True)
    scale_rows = lax.rsqrt(squares / D + eps_norm)
    rows_out[:, :D] = (hidden_out[...] * scale_rows * gain_ref[...].astype(jnp.float32)).astype(jnp.bfloat16)
    logits = logits_ref[...]
    terms = jnp.exp(logits - jnp.max(logits, axis=1, keepdims=True))
    route = terms / jnp.sum(terms, axis=1, keepdims=True)
    lanes = lax.broadcasted_iota(jnp.int32, (ids_ref.shape[0], LANES), 1)
    shares = jnp.zeros(lanes.shape, jnp.float32)
    for k in range(TOPK):
        shares = shares + jnp.where(lanes % HALF_LANES == ids_ref[:, k : k + 1], route[:, k : k + 1], 0.0)
    high = shares.astype(jnp.bfloat16).astype(jnp.float32)
    rows_out[:, D:] = jnp.where(lanes < HALF_LANES, high, shares - high).astype(jnp.bfloat16)


def norm_call(where, mine, other, residual, gain, ids, logits):
    vmem, smem = pl.BlockSpec(memory_space=pltpu.VMEM), pl.BlockSpec(memory_space=pltpu.SMEM)
    rows = residual.shape[0]
    return pl.pallas_call(
        norm_kernel,
        out_shape=[
            jax.ShapeDtypeStruct((rows, D), jnp.float32),
            jax.ShapeDtypeStruct((rows, D + LANES), jnp.bfloat16),
        ],
        in_specs=[smem] + [vmem] * 6,
        out_specs=[vmem] * 2,
        compiler_params=pltpu.CompilerParams(vmem_limit_bytes=SMALL_LIMIT),
    )(where, mine, other, residual, gain, ids, logits)


def pieces_of(width, step):
    return [(at, min(step, width - at)) for at in range(0, width, step)]


def silu(value):
    return value / (1.0 + jnp.exp(-value))


def hold_kernel(n, *refs):
    done_ref, sems = refs[2 * n], refs[2 * n + 1]
    done_ref[...] = jnp.zeros_like(done_ref)
    copies = [pltpu.make_async_copy(refs[i].at[0], refs[n + i], sems.at[i]) for i in range(n)]
    for copy in copies:
        copy.start()
    for copy in copies:
        copy.wait()


def hold_call(arrays):
    n = len(arrays)
    return pl.pallas_call(
        functools.partial(hold_kernel, n),
        out_shape=[pltpu.VMEM(a.shape[1:], a.dtype) for a in arrays] + [jax.ShapeDtypeStruct((8, 128), jnp.float32)],
        in_specs=[pl.BlockSpec(memory_space=pltpu.HBM)] * n,
        out_specs=[pl.BlockSpec(memory_space=pltpu.VMEM)] * (n + 1),
        scratch_shapes=[pltpu.SemaphoreType.DMA((n,))],
        compiler_params=pltpu.CompilerParams(vmem_limit_bytes=HOLD_LIMIT),
        cost_estimate=SMALL_COST,
    )(*arrays)


def stack_kernel(n, *refs):
    out_ref, sems = refs[n], refs[n + 1]
    copies = [pltpu.make_async_copy(refs[i], out_ref.at[i], sems.at[i]) for i in range(n)]
    for copy in copies:
        copy.start()
    for copy in copies:
        copy.wait()


def stack_call(arrays):
    n = len(arrays)
    return pl.pallas_call(
        functools.partial(stack_kernel, n),
        out_shape=jax.ShapeDtypeStruct((n,) + arrays[0].shape, arrays[0].dtype),
        in_specs=[pl.BlockSpec(memory_space=pl.ANY)] * n,
        out_specs=pl.BlockSpec(memory_space=pl.ANY),
        scratch_shapes=[pltpu.SemaphoreType.DMA((n,))],
        compiler_params=pltpu.CompilerParams(vmem_limit_bytes=ASSEMBLE_LIMIT),
        cost_estimate=SMALL_COST,
    )(*arrays)


def log_kernel(where_ref, mine_ref, other_ref, out_ref):
    rows = mine_ref.shape[0]
    for i, part in enumerate((mine_ref, other_ref)):
        at = lax.rem(where_ref[3] + i, CORES) * rows
        out_ref[pl.ds(pl.multiple_of(at, rows), rows), :] = part[...]


def log_call(where, mine, other):
    vmem, smem = pl.BlockSpec(memory_space=pltpu.VMEM), pl.BlockSpec(memory_space=pltpu.SMEM)
    return pl.pallas_call(
        log_kernel,
        out_shape=jax.ShapeDtypeStruct((CORES * mine.shape[0], mine.shape[1]), jnp.float32),
        in_specs=[smem, vmem, vmem],
        out_specs=vmem,
        compiler_params=pltpu.CompilerParams(vmem_limit_bytes=ASSEMBLE_LIMIT),
        cost_estimate=SMALL_COST,
    )(where, mine, other)


def assemble_kernel(n_z, n_x, parities, n, where_ref, *refs):
    out_ref, sems = refs[n], refs[n + 1]
    units, width = refs[0].shape[3:]
    copies = []
    for k in range(n):
        for s in range(n_z):
            for i in range(n_x):
                source = source_of(where_ref, n_z, n_x, s, i, k % parities)
                lanes = pl.ds(pl.multiple_of(source // (CORES // parities) * width, LANES), width)
                target = out_ref.at[:, pl.ds(k // parities * units, units), lanes]
                copies.append(pltpu.make_async_copy(refs[k].at[s, i], target, sems.at[len(copies)]))
    for copy in copies:
        copy.start()
    for copy in copies:
        copy.wait()


def assemble_call(where, parts):
    n_z, n_x, three, units, width = parts[0][0].shape
    parities = len(parts[0])
    if width < LANES:
        parities, width = 1, CORES * width
        flip = where[3] == 0
        parts = [[jnp.where(flip, jnp.concatenate(p, axis=-1), jnp.concatenate(p[::-1], axis=-1))] for p in parts]
    operands = [a for p in parts for a in p]
    n = len(operands)
    return pl.pallas_call(
        functools.partial(assemble_kernel, n_z, n_x, parities, n),
        out_shape=pltpu.VMEM((three, len(parts) * units, D), operands[0].dtype),
        in_specs=[pl.BlockSpec(memory_space=pltpu.SMEM)] + [pl.BlockSpec(memory_space=pl.ANY)] * n,
        out_specs=pl.BlockSpec(memory_space=pltpu.VMEM),
        scratch_shapes=[pltpu.SemaphoreType.DMA((n * n_z * n_x,))],
        compiler_params=pltpu.CompilerParams(vmem_limit_bytes=ASSEMBLE_LIMIT),
        cost_estimate=SMALL_COST,
    )(where, *operands)


def experts_kernel(n_z, n_blocks, up_step, down_step, *refs):
    where_ref = refs[0]
    x_in = refs[1 : 1 + n_blocks]
    refs = refs[1 + n_blocks :]
    experts = [refs[3 * e : 3 * e + 3] for e in range(CORES)]
    refs = refs[3 * CORES + 1 :]
    outs, act_scr = refs[:n_blocks], refs[n_blocks]
    rows = x_in[0].shape[0]
    units = act_scr.shape[2]
    shares = jnp.concatenate([x[:, D:] for x in x_in], axis=0).astype(jnp.float32)
    lanes = lax.broadcasted_iota(jnp.int32, shares.shape, 1) % HALF_LANES
    x = jnp.concatenate([x[:, :D] for x in x_in], axis=0)
    for e in range(CORES):
        expert = source_of(where_ref, n_z, n_blocks, 0, 0, e)
        scale = jnp.sum(jnp.where(lanes == expert, shares, 0.0), axis=1, keepdims=True)
        for at, size in pieces_of(units, up_step):
            gate = jnp.dot(x, experts[e][0][:, at : at + size], preferred_element_type=jnp.float32)
            up = jnp.dot(x, experts[e][1][:, at : at + size], preferred_element_type=jnp.float32)
            act_scr[e, :, at : at + size] = (silu(gate) * up * scale).astype(jnp.bfloat16)
    for at, size in pieces_of(D, down_step):
        part = 0.0
        for e in range(CORES):
            part = part + jnp.dot(act_scr[e], experts[e][2][:, at : at + size], preferred_element_type=jnp.float32)
        part = part.astype(jnp.bfloat16)
        for j in range(n_blocks):
            outs[j][:, at : at + size] = part[j * rows : (j + 1) * rows, :]


def experts_call(where, n_z, blocks, weights, held_done):
    rows, n_blocks = blocks[0].shape[0], len(blocks)
    units = weights[0].shape[1]
    vmem, smem = pl.BlockSpec(memory_space=pltpu.VMEM), pl.BlockSpec(memory_space=pltpu.SMEM)
    return pl.pallas_call(
        functools.partial(experts_kernel, n_z, n_blocks, 512, 512),
        out_shape=[jax.ShapeDtypeStruct((rows, D), jnp.bfloat16)] * n_blocks,
        in_specs=[smem] + [vmem] * (n_blocks + len(weights)) + [pl.BlockSpec(memory_space=pl.ANY)],
        out_specs=[vmem] * n_blocks,
        scratch_shapes=[pltpu.VMEM((CORES, n_blocks * rows, units), jnp.bfloat16)],
        compiler_params=pltpu.CompilerParams(vmem_limit_bytes=EXPERT_LIMIT),
        cost_estimate=SMALL_COST,
    )(where, *blocks, *weights, held_done)


def shared_kernel(n_blocks, down_step, *refs):
    x_in, sums_in = refs[:n_blocks], refs[n_blocks : 2 * n_blocks]
    shared_ref = refs[2 * n_blocks]
    outs = refs[2 * n_blocks + 1 :]
    rows = x_in[0].shape[0]
    x = jnp.concatenate([x[:, :D] for x in x_in], axis=0)
    across = (((1,), (1,)), ((), ()))
    gate = lax.dot_general(x, shared_ref[0], across, preferred_element_type=jnp.float32)
    up = lax.dot_general(x, shared_ref[1], across, preferred_element_type=jnp.float32)
    act = (silu(gate) * up).astype(jnp.bfloat16)
    for at, size in pieces_of(D, down_step):
        part = jnp.dot(act, shared_ref[2, :, at : at + size], preferred_element_type=jnp.float32)
        for j in range(n_blocks):
            total = part[j * rows : (j + 1) * rows, :] + sums_in[j][:, at : at + size].astype(jnp.float32)
            outs[j][:, at : at + size] = total.astype(jnp.bfloat16)


def shared_call(blocks, sums, shared):
    rows, n_blocks = blocks[0].shape[0], len(blocks)
    vmem = pl.BlockSpec(memory_space=pltpu.VMEM)
    return pl.pallas_call(
        functools.partial(shared_kernel, n_blocks, 512),
        out_shape=[jax.ShapeDtypeStruct((rows, D), jnp.bfloat16)] * n_blocks,
        in_specs=[vmem] * (2 * n_blocks + 1),
        out_specs=[vmem] * n_blocks,
        compiler_params=pltpu.CompilerParams(vmem_limit_bytes=EXPERT_LIMIT),
        cost_estimate=SMALL_COST,
    )(*blocks, *sums, shared)


def sum_kernel(n, *refs):
    total = refs[0][...].astype(jnp.float32)
    for ref in refs[1:n]:
        total = total + ref[...].astype(jnp.float32)
    refs[n][...] = total.astype(jnp.bfloat16)


def sum_call(values):
    n = len(values)
    vmem = pl.BlockSpec(memory_space=pltpu.VMEM)
    return pl.pallas_call(
        functools.partial(sum_kernel, n),
        out_shape=jax.ShapeDtypeStruct(values[0].shape, jnp.bfloat16),
        in_specs=[vmem] * n,
        out_specs=vmem,
        compiler_params=pltpu.CompilerParams(vmem_limit_bytes=EXPERT_LIMIT),
        cost_estimate=SMALL_COST,
    )(*values)


def pages_kernel(n_groups, n_columns, where_ref, table_ref, *refs):
    sources, out_ref = refs[:n_groups], refs[n_groups]
    pages_dev = out_ref.shape[0]
    first = where_ref[0] * pages_dev
    for i in range(n_groups):
        group = lax.rem(where_ref[4] + n_groups - i, n_groups)
        for j in range(pages_dev):
            slot = table_ref[group, first + j] - (where_ref[4] * n_columns * pages_dev + first)

            @pl.when((slot >= 0) & (slot < pages_dev))
            def _():
                out_ref[slot] = sources[i][j]


def pages_call(where, n_columns, table, sources):
    vmem, smem = pl.BlockSpec(memory_space=pltpu.VMEM), pl.BlockSpec(memory_space=pltpu.SMEM)
    return pl.pallas_call(
        functools.partial(pages_kernel, len(sources), n_columns),
        out_shape=jax.ShapeDtypeStruct(sources[0].shape, jnp.bfloat16),
        in_specs=[smem, smem] + [vmem] * len(sources),
        out_specs=vmem,
        compiler_params=pltpu.CompilerParams(vmem_limit_bytes=SMALL_LIMIT),
    )(where, table, *sources)


def on_device(
    queries,
    keys_then_values,
    residual,
    norm_gain,
    prompt_lengths,
    expert_ids,
    router_logits,
    w_gate,
    w_up,
    w_down,
    w_shared_gate,
    w_shared_up,
    w_shared_down,
    page_table,
):
    token_rows = queries.shape[0]
    n_groups = lax.axis_size("req")
    n_columns = lax.axis_size("exp")
    column = lax.axis_index("exp")
    my_group = lax.axis_index("req")
    n_z, n_x = Z_SIZE, n_columns // (Z_SIZE * CORES)
    my_z, my_x, my_c = column // (n_x * CORES), (column // CORES) % n_x, column % CORES
    where = jnp.stack([column, my_z, my_x, my_c, my_group]).astype(jnp.int32)
    after = lax.optimization_barrier

    def hop(value, dz=0, dx=0, dc=0):
        pairs = [
            (place_of(n_x, z, x, c), place_of(n_x, (z + dz) % n_z, (x + dx) % n_x, (c + dc) % CORES))
            for z in range(n_z)
            for x in range(n_x)
            for c in range(CORES)
        ]
        return lax.ppermute(value, "exp", pairs)

    def hop_group(value, i):
        return lax.ppermute(value, "req", [(g, (g + i) % n_groups) for g in range(n_groups)])

    def across_x(value):
        return [value] + [hop(value, dx=i) for i in range(1, n_x)]

    def pick(value, at, axis):
        return lax.dynamic_index_in_dim(value, at, axis, keepdims=False)

    width = D // CORES
    kv_width = KEY_VALUE_HEADS // CORES * HEAD_SIZE
    kv_pair = keys_then_values.reshape(token_rows, 2, KEY_VALUE_HEADS * HEAD_SIZE)
    kv_mine, kv_other = [
        lax.dynamic_slice_in_dim(kv_pair, c * kv_width, kv_width, 2).reshape(token_rows, 2 * kv_width)
        for c in (my_c, 1 - my_c)
    ]
    kv_got = hop(kv_other, dc=1)

    units = w_shared_gate.shape[1] // (n_z * n_x)
    split = [w.T.reshape(n_z, n_x, units, w.shape[0]) for w in (w_shared_gate, w_shared_up, w_shared_down)]
    split = jnp.pad(jnp.stack(split, axis=2), ((0, 0), (0, 0), (0, 0), (0, -units % 16), (0, 0)))
    split = [pick(split, (my_x + i) % n_x, 1) for i in range(n_x)]
    split, kv_mine, kv_got = after((split, kv_mine, kv_got))
    split = [split[0]] + [hop(split[i], dx=i) for i in range(1, n_x)]

    kv_chip = jnp.concatenate([kv_mine, kv_got], axis=0)
    q_source, kv_chip = after((queries, kv_chip))
    q_mine, q_other = [lax.dynamic_slice_in_dim(q_source, c * width, width, 1) for c in (my_c, 1 - my_c)]
    q_chip = [q_mine, hop(q_other, dc=1)]

    own_weights, other_weights = [w_gate, w_up, w_down], []
    own_weights, q_chip = after((own_weights, q_chip))
    kv_blocks, state, across = [], None, None

    def attend(s, state):
        return attention_call(where, n_z, s, prompt_lengths, q_chip, kv_blocks[s], state)

    newest = kv_chip
    for s in range(n_z):
        before, across = across, [hop(newest, dx=i) for i in range(1, n_x)]
        onward = hop(newest, dz=1) if s < n_z - 1 else None
        if s == 0:
            split, onward, q_chip = after((split, onward, q_chip))
            split = jnp.stack(split, axis=1)
            turned = [pick(split, (my_z + i) % n_z, 0) for i in range(n_z)]
        elif s < n_z - 1:
            if s > 1:
                state = attend(s - 2, state)
                near = hop(turned[1], dz=1)
                state, near, onward = after((state, near, onward))
            before, onward, other_weights = after((before, onward, other_weights))
        else:
            state = attend(s - 2, state)
            far = hop(turned[3], dz=3)
            middle = hop(turned[2], dz=2)
            before, across, state, far, other_weights = after((before, across, state, far, other_weights))
        if s > 0:
            kv_blocks.append([newest_before] + before)
        if s < len(own_weights):
            source, onward = after((own_weights[s], onward))
            other_weights.append(hop(source, dc=1))
        newest_before, newest = newest, onward
    state = attend(n_z - 2, state)
    kv_blocks.append([newest_before] + across)
    state = attend(n_z - 1, state)
    attn_mine, attn_other, log_mine, log_other = state
    attn_got, middle = after((hop(attn_other, dc=1), middle))
    hidden, rows = norm_call(
        where, attn_mine, attn_got, residual, norm_gain.reshape(1, D), expert_ids, router_logits
    )

    def across_x(outs):
        return [hop(outs[i], dx=-i) for i in range(1, n_x)]

    row_blocks, sums = [], []
    newest, weights = after((rows, own_weights + other_weights))
    for s in range(n_z):
        if s < n_z - 1:
            blocks = [newest] + [hop(newest, dx=i) for i in range(1, n_x)]
            onward = hop(newest, dz=1)
        else:
            blocks = [newest] + [hop(b, dz=1) for b in row_blocks[-1][1:]]
        if s == 0:
            shared = stack_call([turned[0], near, middle, far])
            shared, weights = after((shared, weights))
            shared_near = hop(shared, dc=1)
            shared_far = [hop_group(shared, i) for i in range(1, n_groups)]
            *held_weights, held_done = hold_call(weights)
            blocks, onward, held_done, shared_near = after((blocks, onward, held_done, shared_near))
        elif s < n_z - 1:
            sums.append(experts_call(where, n_z, row_blocks[s - 1], held_weights, held_done))
            if s == 1:
                blocks, onward, sums, shared_far = after((blocks, onward, sums, shared_far))
                shared_far = [[p, hop(p, dc=1)] for p in shared_far]
            else:
                blocks, onward, sums, shared_far = after((blocks, onward, sums, shared_far))
        row_blocks.append(blocks)
        newest = onward
    parts = [[shared, shared_near]] + shared_far
    shared = assemble_call(where, parts)

    def with_shared(s):
        outs = shared_call(row_blocks[s], sums[s], shared)
        return outs[0], [hop(outs[i], dx=-i) for i in range(1, n_x)]

    def experts_of(s):
        return experts_call(where, n_z, row_blocks[s], held_weights, held_done)

    mine_1, back_1 = with_shared(1)
    mine_1, row_blocks[2] = after((mine_1, row_blocks[2]))
    sums.append(experts_of(2))
    mine_2, back_2 = with_shared(2)
    mine_1, back_1, mine_2 = after((mine_1, back_1, mine_2))
    total = sum_call([mine_1] + back_1)
    total, row_blocks[3] = after((total, row_blocks[3]))
    ring = hop(total, dz=1)
    sums.append(experts_of(3))
    mine_3, back_3 = with_shared(3)
    mine_3, sums[0] = after((mine_3, sums[0]))
    mine_0, back_0 = with_shared(0)
    mine_2, back_2, ring, mine_0 = after((mine_2, back_2, ring, mine_0))
    ring = hop(sum_call([mine_2] + back_2 + [ring]), dz=1)
    ring = hop(sum_call([mine_3] + back_3 + [ring]), dz=1)

    pages_dev = token_rows // PAGE
    own_pages = keys_then_values.reshape(pages_dev, PAGE, keys_then_values.shape[1])
    own_pages, log_other, mine_0 = after((own_pages, log_other, mine_0))
    page_sources = [own_pages] + [hop_group(own_pages, i) for i in range(1, n_groups)]
    log_got = hop(log_other, dc=1)
    kv_cache = pages_call(where, n_columns, page_table, page_sources)
    log_totals = log_call(where, log_mine, log_got)

    layer_out = hidden
    for term in [mine_0] + back_0 + [ring]:
        layer_out = layer_out + term.astype(jnp.float32)
    layer_out = layer_out.astype(jnp.bfloat16)
    return (layer_out, kv_cache, log_totals)


def solution(mesh):
    placed = (
        P(("req", "exp"), None),
        P(("req", "exp"), None),
        P(("req", "exp"), None),
        P(),
        P("req", None),
        P(("req", "exp"), None),
        P(("req", "exp"), None),
        P("exp", None, None),
        P("exp", None, None),
        P("exp", None, None),
        P("exp", "req"),
        P("exp", "req"),
        P("exp", "req"),
        P(),
    )
    return jax.shard_map(
        on_device,
        mesh=mesh,
        in_specs=placed,
        out_specs=(P(("req", "exp"), None), P(("req", "exp"), None, None), P(None, ("req", "exp"))),
        check_vma=False,
    )
```

```python
import functools
import math

import jax
import jax.numpy as jnp
from jax import lax
from jax.experimental import pallas as pl
from jax.experimental.pallas import tpu as pltpu
from jax.sharding import PartitionSpec as P

D = 2048
QUERY_HEADS = 16
KEY_VALUE_HEADS = 4
HEAD_SIZE = 128
TOPK = 6
PAGE = 16
CORES = 2
Z_SIZE = 4

large_negative = -1e30
eps_norm = 1e-06
SMALL_LIMIT = 14 * 1024 * 1024
EXPERT_LIMIT = 8 * 1024 * 1024
ASSEMBLE_LIMIT = 2 * 1024 * 1024
HOLD_LIMIT = 16 * 1024 * 1024
LANES = 128
HALF_LANES = 64
SMALL_COST = pl.CostEstimate(flops=1000, bytes_accessed=1000, transcendentals=0)
SCORE_SCALE = HEAD_SIZE ** (-0.5)
EXP2_SCALE = SCORE_SCALE * math.log2(math.e)


def place_of(n_x, z, x, c):
    return (z * n_x + x) * CORES + c


def source_of(where_ref, n_z, n_x, s, i, parity):
    z = lax.rem(where_ref[1] + n_z - s, n_z)
    x = lax.rem(where_ref[2] + n_x - i, n_x)
    return place_of(n_x, z, x, lax.rem(where_ref[3] + parity, CORES))


def attention_kernel(first, last, n_z, n_x, s, *refs):
    refs = list(refs)
    where_ref, lengths_ref = refs[:2]
    n_blocks = n_x
    queries = refs[2 : 2 + CORES]
    blocks = refs[2 + CORES : 2 + CORES + n_blocks]
    refs = refs[2 + CORES + n_blocks :]
    if not first:
        acc_in, max_in, sum_in = refs[:3]
        refs = refs[3:]
    rows = queries[0].shape[0]
    kv_heads = KEY_VALUE_HEADS // CORES
    heads = QUERY_HEADS // KEY_VALUE_HEADS
    wide = CORES * rows
    iota = lax.broadcasted_iota(jnp.int32, (1, rows), 1)
    query_pos = jnp.concatenate(
        [source_of(where_ref, n_z, n_x, 0, 0, i) * rows + iota for i in range(CORES)], axis=1
    )
    start = jnp.zeros((1, wide), jnp.int32)
    end = jnp.int32(0)
    for i in range(lengths_ref.shape[1]):
        end = end + lengths_ref[0, i]
        start = start + jnp.where(query_pos >= end, lengths_ref[0, i], 0)
    biases = []
    for j in range(n_blocks * CORES):
        key_pos = source_of(where_ref, n_z, n_x, s, j // CORES, j % CORES) * rows
        key_pos = key_pos + lax.broadcasted_iota(jnp.int32, (rows, wide), 0)
        visible = (key_pos >= start) & (key_pos <= query_pos)
        biases.append(jnp.where(visible, 0.0, large_negative))
    bias = jnp.concatenate(biases, axis=0)
    bias = jnp.concatenate([bias] * heads, axis=1)
    for h in range(kv_heads):
        columns = slice(h * HEAD_SIZE, (h + 1) * HEAD_SIZE)
        value_columns = slice((kv_heads + h) * HEAD_SIZE, (kv_heads + h + 1) * HEAD_SIZE)
        keys = jnp.concatenate([b[:, columns] for b in blocks], axis=0)
        values = jnp.concatenate([b[:, value_columns] for b in blocks], axis=0)
        query = jnp.concatenate(
            [
                q[:, (h * heads + g) * HEAD_SIZE : (h * heads + g + 1) * HEAD_SIZE]
                for g in range(heads)
                for q in queries
            ],
            axis=0,
        )
        scores = lax.dot_general(keys, query, (((1,), (1,)), ((), ())), preferred_element_type=jnp.float32)
        scores = scores + bias
        new_max = jnp.max(scores, axis=0, keepdims=True)
        if not first:
            old_max = max_in[h : h + 1, :]
            new_max = jnp.maximum(new_max, old_max)
            fade = jnp.exp2((old_max - new_max) * EXP2_SCALE)
        terms = jnp.exp2((scores - new_max) * EXP2_SCALE)
        total = jnp.sum(terms, axis=0, keepdims=True)
        mixed = lax.dot_general(
            values, terms.astype(jnp.bfloat16), (((0,), (0,)), ((), ())), preferred_element_type=jnp.float32
        )
        if not first:
            total = total + fade * sum_in[h : h + 1, :]
            mixed = mixed + fade * acc_in[h]
        if last:
            mixed = mixed / total
            log_row = new_max * SCORE_SCALE + jnp.log(total)
            for g in range(heads):
                for i in range(CORES):
                    part = slice(g * wide + i * rows, g * wide + (i + 1) * rows)
                    at = h * heads + g
                    refs[i][:, at * HEAD_SIZE : (at + 1) * HEAD_SIZE] = mixed[:, part].T.astype(jnp.bfloat16)
                    refs[CORES + i][at : at + 1, :] = log_row[:, part]
        else:
            refs[0][h] = mixed
            refs[1][h : h + 1, :] = new_max
            refs[2][h : h + 1, :] = total


def attention_call(where, n_z, s, lengths, queries, blocks, state):
    rows, columns = queries[0].shape
    last = s == n_z - 1
    kv_heads = KEY_VALUE_HEADS // CORES
    wide = CORES * rows * (QUERY_HEADS // KEY_VALUE_HEADS)
    vmem, smem = pl.BlockSpec(memory_space=pltpu.VMEM), pl.BlockSpec(memory_space=pltpu.SMEM)
    operands = [where, lengths, *queries, *blocks] + ([] if state is None else list(state))
    if last:
        outs = [jax.ShapeDtypeStruct((rows, columns), jnp.bfloat16)] * CORES
        outs += [jax.ShapeDtypeStruct((QUERY_HEADS // CORES, rows), jnp.float32)] * CORES
    else:
        outs = [jax.ShapeDtypeStruct((kv_heads, HEAD_SIZE, wide), jnp.float32)]
        outs += [jax.ShapeDtypeStruct((kv_heads, wide), jnp.float32)] * 2
    keys = sum(b.shape[0] for b in blocks)
    return pl.pallas_call(
        functools.partial(attention_kernel, state is None, last, n_z, len(blocks), s),
        out_shape=outs,
        in_specs=[smem, smem] + [vmem] * (len(operands) - 2),
        out_specs=[vmem] * len(outs),
        compiler_params=pltpu.CompilerParams(vmem_limit_bytes=SMALL_LIMIT),
        cost_estimate=SMALL_COST,
    )(*operands)


def norm_kernel(where_ref, mine_ref, other_ref, residual_ref, gain_ref, ids_ref, logits_ref, hidden_out, rows_out):
    width = mine_ref.shape[1]
    squares = 0.0
    for i, part in enumerate((mine_ref, other_ref)):
        span = pl.ds(pl.multiple_of(lax.rem(where_ref[3] + i, CORES) * width, width), width)
        hidden = residual_ref[:, span].astype(jnp.float32) + part[...].astype(jnp.float32)
        hidden_out[:, span] = hidden
        squares = squares + jnp.sum(hidden * hidden, axis=-1, keepdims=True)
    scale_rows = lax.rsqrt(squares / D + eps_norm)
    rows_out[:, :D] = (hidden_out[...] * scale_rows * gain_ref[...].astype(jnp.float32)).astype(jnp.bfloat16)
    logits = logits_ref[...]
    terms = jnp.exp(logits - jnp.max(logits, axis=1, keepdims=True))
    route = terms / jnp.sum(terms, axis=1, keepdims=True)
    lanes = lax.broadcasted_iota(jnp.int32, (ids_ref.shape[0], LANES), 1)
    shares = jnp.zeros(lanes.shape, jnp.float32)
    for k in range(TOPK):
        shares = shares + jnp.where(lanes % HALF_LANES == ids_ref[:, k : k + 1], route[:, k : k + 1], 0.0)
    high = shares.astype(jnp.bfloat16).astype(jnp.float32)
    rows_out[:, D:] = jnp.where(lanes < HALF_LANES, high, shares - high).astype(jnp.bfloat16)


def norm_call(where, mine, other, residual, gain, ids, logits):
    vmem, smem = pl.BlockSpec(memory_space=pltpu.VMEM), pl.BlockSpec(memory_space=pltpu.SMEM)
    rows = residual.shape[0]
    return pl.pallas_call(
        norm_kernel,
        out_shape=[
            jax.ShapeDtypeStruct((rows, D), jnp.float32),
            jax.ShapeDtypeStruct((rows, D + LANES), jnp.bfloat16),
        ],
        in_specs=[smem] + [vmem] * 6,
        out_specs=[vmem] * 2,
        compiler_params=pltpu.CompilerParams(vmem_limit_bytes=SMALL_LIMIT),
    )(where, mine, other, residual, gain, ids, logits)


def pieces_of(width, step):
    return [(at, min(step, width - at)) for at in range(0, width, step)]


def silu(value):
    return value / (1.0 + jnp.exp(-value))


def hold_kernel(n, *refs):
    done_ref, sems = refs[2 * n], refs[2 * n + 1]
    done_ref[...] = jnp.zeros_like(done_ref)
    copies = [pltpu.make_async_copy(refs[i].at[0], refs[n + i], sems.at[i]) for i in range(n)]
    for copy in copies:
        copy.start()
    for copy in copies:
        copy.wait()


def hold_call(arrays):
    n = len(arrays)
    return pl.pallas_call(
        functools.partial(hold_kernel, n),
        out_shape=[pltpu.VMEM(a.shape[1:], a.dtype) for a in arrays] + [jax.ShapeDtypeStruct((8, 128), jnp.float32)],
        in_specs=[pl.BlockSpec(memory_space=pltpu.HBM)] * n,
        out_specs=[pl.BlockSpec(memory_space=pltpu.VMEM)] * (n + 1),
        scratch_shapes=[pltpu.SemaphoreType.DMA((n,))],
        compiler_params=pltpu.CompilerParams(vmem_limit_bytes=HOLD_LIMIT),
        cost_estimate=SMALL_COST,
    )(*arrays)


def stack_kernel(n, *refs):
    out_ref, sems = refs[n], refs[n + 1]
    copies = [pltpu.make_async_copy(refs[i], out_ref.at[i], sems.at[i]) for i in range(n)]
    for copy in copies:
        copy.start()
    for copy in copies:
        copy.wait()


def stack_call(arrays):
    n = len(arrays)
    return pl.pallas_call(
        functools.partial(stack_kernel, n),
        out_shape=jax.ShapeDtypeStruct((n,) + arrays[0].shape, arrays[0].dtype),
        in_specs=[pl.BlockSpec(memory_space=pl.ANY)] * n,
        out_specs=pl.BlockSpec(memory_space=pl.ANY),
        scratch_shapes=[pltpu.SemaphoreType.DMA((n,))],
        compiler_params=pltpu.CompilerParams(vmem_limit_bytes=ASSEMBLE_LIMIT),
        cost_estimate=SMALL_COST,
    )(*arrays)


def log_kernel(where_ref, mine_ref, other_ref, out_ref):
    rows = mine_ref.shape[0]
    for i, part in enumerate((mine_ref, other_ref)):
        at = lax.rem(where_ref[3] + i, CORES) * rows
        out_ref[pl.ds(pl.multiple_of(at, rows), rows), :] = part[...]


def log_call(where, mine, other):
    vmem, smem = pl.BlockSpec(memory_space=pltpu.VMEM), pl.BlockSpec(memory_space=pltpu.SMEM)
    return pl.pallas_call(
        log_kernel,
        out_shape=jax.ShapeDtypeStruct((CORES * mine.shape[0], mine.shape[1]), jnp.float32),
        in_specs=[smem, vmem, vmem],
        out_specs=vmem,
        compiler_params=pltpu.CompilerParams(vmem_limit_bytes=ASSEMBLE_LIMIT),
        cost_estimate=SMALL_COST,
    )(where, mine, other)


def assemble_kernel(n_z, n_x, parities, n, where_ref, *refs):
    out_ref, sems = refs[n], refs[n + 1]
    units, width = refs[0].shape[3:]
    copies = []
    for k in range(n):
        for s in range(n_z):
            for i in range(n_x):
                source = source_of(where_ref, n_z, n_x, s, i, k % parities)
                lanes = pl.ds(pl.multiple_of(source // (CORES // parities) * width, LANES), width)
                target = out_ref.at[:, pl.ds(k // parities * units, units), lanes]
                copies.append(pltpu.make_async_copy(refs[k].at[s, i], target, sems.at[len(copies)]))
    for copy in copies:
        copy.start()
    for copy in copies:
        copy.wait()


def assemble_call(where, parts):
    n_z, n_x, three, units, width = parts[0][0].shape
    parities = len(parts[0])
    if width < LANES:
        parities, width = 1, CORES * width
        flip = where[3] == 0
        parts = [[jnp.where(flip, jnp.concatenate(p, axis=-1), jnp.concatenate(p[::-1], axis=-1))] for p in parts]
    operands = [a for p in parts for a in p]
    n = len(operands)
    return pl.pallas_call(
        functools.partial(assemble_kernel, n_z, n_x, parities, n),
        out_shape=pltpu.VMEM((three, len(parts) * units, D), operands[0].dtype),
        in_specs=[pl.BlockSpec(memory_space=pltpu.SMEM)] + [pl.BlockSpec(memory_space=pl.ANY)] * n,
        out_specs=pl.BlockSpec(memory_space=pltpu.VMEM),
        scratch_shapes=[pltpu.SemaphoreType.DMA((n * n_z * n_x,))],
        compiler_params=pltpu.CompilerParams(vmem_limit_bytes=ASSEMBLE_LIMIT),
        cost_estimate=SMALL_COST,
    )(where, *operands)


def experts_kernel(n_z, n_blocks, slots, up_step, down_step, *refs):
    where_ref = refs[0]
    x_in = refs[1 : 1 + n_blocks]
    refs = refs[1 + n_blocks :]
    experts = [refs[3 * e : 3 * e + 3] for e in range(CORES)]
    refs = refs[3 * CORES + 1 :]
    outs, x_scr, act_scr = refs[:n_blocks], refs[n_blocks], refs[n_blocks + 1]
    rows = x_in[0].shape[0]
    units = act_scr.shape[2]
    lane = lax.broadcasted_iota(jnp.int32, (rows, LANES), 1)
    earlier = (lax.broadcasted_iota(jnp.int32, (rows, rows), 1) < lax.broadcasted_iota(jnp.int32, (rows, rows), 0))
    earlier = earlier.astype(jnp.float32).astype(jnp.bfloat16)
    mine = [source_of(where_ref, n_z, n_blocks, 0, 0, e) for e in range(CORES)]
    scales, puts = [[] for _ in mine], []
    for j in range(n_blocks):
        shares = x_in[j][:, D:]
        picks = []
        for e in range(CORES):
            own = jnp.where(lane % HALF_LANES == mine[e], shares.astype(jnp.float32), 0.0)
            chosen = jnp.sum(own, axis=1, keepdims=True) != 0.0
            chosen = jnp.where(chosen, 1.0, 0.0) + jnp.zeros((rows, LANES), jnp.float32)
            rank = jnp.dot(earlier, chosen.astype(jnp.bfloat16), preferred_element_type=jnp.float32)
            picks.append(jnp.where(rank == lane.astype(jnp.float32), chosen, 0.0))
        puts.append(jnp.concatenate([pick[:, :slots] for pick in picks], axis=1).astype(jnp.bfloat16))
        take = jnp.concatenate([pick.T[:slots] for pick in picks], axis=0).astype(jnp.bfloat16)
        taken = jnp.dot(take, x_in[j][:, :D], preferred_element_type=jnp.float32).astype(jnp.bfloat16)
        taken_shares = jnp.dot(take, shares, preferred_element_type=jnp.float32)
        for e in range(CORES):
            part = slice(e * slots, (e + 1) * slots)
            x_scr[e, j * slots : (j + 1) * slots, :] = taken[part]
            own = lax.broadcasted_iota(jnp.int32, (slots, LANES), 1) % HALF_LANES == mine[e]
            scales[e].append(jnp.sum(jnp.where(own, taken_shares[part], 0.0), axis=1, keepdims=True))
    for e in range(CORES):
        x = x_scr[e]
        scale = jnp.concatenate(scales[e], axis=0)
        for at, size in pieces_of(units, up_step):
            gate = jnp.dot(x, experts[e][0][:, at : at + size], preferred_element_type=jnp.float32)
            up = jnp.dot(x, experts[e][1][:, at : at + size], preferred_element_type=jnp.float32)
            act_scr[e, :, at : at + size] = (silu(gate) * up * scale).astype(jnp.bfloat16)
    for at, size in pieces_of(D, down_step):
        parts = [
            jnp.dot(act_scr[e], experts[e][2][:, at : at + size], preferred_element_type=jnp.float32).astype(jnp.bfloat16)
            for e in range(CORES)
        ]
        for j in range(n_blocks):
            both = jnp.concatenate([part[j * slots : (j + 1) * slots] for part in parts], axis=0)
            outs[j][:, at : at + size] = jnp.dot(puts[j], both, preferred_element_type=jnp.float32).astype(jnp.bfloat16)


def experts_call(where, n_z, blocks, weights, held_done):
    rows, n_blocks = blocks[0].shape[0], len(blocks)
    units = weights[0].shape[1]
    experts = n_z * n_blocks * CORES
    capacity = min(rows, 3 * rows * TOPK // (2 * experts))
    slots = capacity + -capacity % 16
    vmem, smem = pl.BlockSpec(memory_space=pltpu.VMEM), pl.BlockSpec(memory_space=pltpu.SMEM)
    return pl.pallas_call(
        functools.partial(experts_kernel, n_z, n_blocks, slots, 512, 512),
        out_shape=[jax.ShapeDtypeStruct((rows, D), jnp.bfloat16)] * n_blocks,
        in_specs=[smem] + [vmem] * (n_blocks + len(weights)) + [pl.BlockSpec(memory_space=pl.ANY)],
        out_specs=[vmem] * n_blocks,
        scratch_shapes=[
            pltpu.VMEM((CORES, n_blocks * slots, D), jnp.bfloat16),
            pltpu.VMEM((CORES, n_blocks * slots, units), jnp.bfloat16),
        ],
        compiler_params=pltpu.CompilerParams(vmem_limit_bytes=EXPERT_LIMIT),
        cost_estimate=SMALL_COST,
    )(where, *blocks, *weights, held_done)


def shared_kernel(n_blocks, down_step, *refs):
    x_in, sums_in = refs[:n_blocks], refs[n_blocks : 2 * n_blocks]
    shared_ref = refs[2 * n_blocks]
    outs = refs[2 * n_blocks + 1 :]
    rows = x_in[0].shape[0]
    x = jnp.concatenate([x[:, :D] for x in x_in], axis=0)
    across = (((1,), (1,)), ((), ()))
    gate = lax.dot_general(x, shared_ref[0], across, preferred_element_type=jnp.float32)
    up = lax.dot_general(x, shared_ref[1], across, preferred_element_type=jnp.float32)
    act = (silu(gate) * up).astype(jnp.bfloat16)
    for at, size in pieces_of(D, down_step):
        part = jnp.dot(act, shared_ref[2, :, at : at + size], preferred_element_type=jnp.float32)
        for j in range(n_blocks):
            total = part[j * rows : (j + 1) * rows, :] + sums_in[j][:, at : at + size].astype(jnp.float32)
            outs[j][:, at : at + size] = total.astype(jnp.bfloat16)


def shared_call(blocks, sums, shared):
    rows, n_blocks = blocks[0].shape[0], len(blocks)
    vmem = pl.BlockSpec(memory_space=pltpu.VMEM)
    return pl.pallas_call(
        functools.partial(shared_kernel, n_blocks, 512),
        out_shape=[jax.ShapeDtypeStruct((rows, D), jnp.bfloat16)] * n_blocks,
        in_specs=[vmem] * (2 * n_blocks + 1),
        out_specs=[vmem] * n_blocks,
        compiler_params=pltpu.CompilerParams(vmem_limit_bytes=EXPERT_LIMIT),
        cost_estimate=SMALL_COST,
    )(*blocks, *sums, shared)


def sum_kernel(n, *refs):
    total = refs[0][...].astype(jnp.float32)
    for ref in refs[1:n]:
        total = total + ref[...].astype(jnp.float32)
    refs[n][...] = total.astype(jnp.bfloat16)


def sum_call(values):
    n = len(values)
    vmem = pl.BlockSpec(memory_space=pltpu.VMEM)
    return pl.pallas_call(
        functools.partial(sum_kernel, n),
        out_shape=jax.ShapeDtypeStruct(values[0].shape, jnp.bfloat16),
        in_specs=[vmem] * n,
        out_specs=vmem,
        compiler_params=pltpu.CompilerParams(vmem_limit_bytes=EXPERT_LIMIT),
        cost_estimate=SMALL_COST,
    )(*values)


def pages_kernel(n_groups, n_columns, where_ref, table_ref, *refs):
    sources, out_ref = refs[:n_groups], refs[n_groups]
    pages_dev = out_ref.shape[0]
    first = where_ref[0] * pages_dev
    for i in range(n_groups):
        group = lax.rem(where_ref[4] + n_groups - i, n_groups)
        for j in range(pages_dev):
            slot = table_ref[group, first + j] - (where_ref[4] * n_columns * pages_dev + first)

            @pl.when((slot >= 0) & (slot < pages_dev))
            def _():
                out_ref[slot] = sources[i][j]


def pages_call(where, n_columns, table, sources):
    vmem, smem = pl.BlockSpec(memory_space=pltpu.VMEM), pl.BlockSpec(memory_space=pltpu.SMEM)
    return pl.pallas_call(
        functools.partial(pages_kernel, len(sources), n_columns),
        out_shape=jax.ShapeDtypeStruct(sources[0].shape, jnp.bfloat16),
        in_specs=[smem, smem] + [vmem] * len(sources),
        out_specs=vmem,
        compiler_params=pltpu.CompilerParams(vmem_limit_bytes=SMALL_LIMIT),
    )(where, table, *sources)


def on_device(
    queries,
    keys_then_values,
    residual,
    norm_gain,
    prompt_lengths,
    expert_ids,
    router_logits,
    w_gate,
    w_up,
    w_down,
    w_shared_gate,
    w_shared_up,
    w_shared_down,
    page_table,
):
    token_rows = queries.shape[0]
    n_groups = lax.axis_size("req")
    n_columns = lax.axis_size("exp")
    column = lax.axis_index("exp")
    my_group = lax.axis_index("req")
    n_z, n_x = Z_SIZE, n_columns // (Z_SIZE * CORES)
    my_z, my_x, my_c = column // (n_x * CORES), (column // CORES) % n_x, column % CORES
    where = jnp.stack([column, my_z, my_x, my_c, my_group]).astype(jnp.int32)
    after = lax.optimization_barrier

    def hop(value, dz=0, dx=0, dc=0):
        pairs = [
            (place_of(n_x, z, x, c), place_of(n_x, (z + dz) % n_z, (x + dx) % n_x, (c + dc) % CORES))
            for z in range(n_z)
            for x in range(n_x)
            for c in range(CORES)
        ]
        return lax.ppermute(value, "exp", pairs)

    def hop_group(value, i):
        return lax.ppermute(value, "req", [(g, (g + i) % n_groups) for g in range(n_groups)])

    def across_x(value):
        return [value] + [hop(value, dx=i) for i in range(1, n_x)]

    def pick(value, at, axis):
        return lax.dynamic_index_in_dim(value, at, axis, keepdims=False)

    width = D // CORES
    kv_width = KEY_VALUE_HEADS // CORES * HEAD_SIZE
    kv_mine, kv_other = [
        jnp.concatenate(
            [
                lax.dynamic_slice_in_dim(keys_then_values, at + c * kv_width, kv_width, 1)
                for at in (0, KEY_VALUE_HEADS * HEAD_SIZE)
            ],
            axis=1,
        )
        for c in (my_c, 1 - my_c)
    ]
    kv_got = hop(kv_other, dc=1)

    units = w_shared_gate.shape[1] // (n_z * n_x)
    split = [w.T.reshape(n_z, n_x, units, w.shape[0]) for w in (w_shared_gate, w_shared_up, w_shared_down)]
    split = jnp.pad(jnp.stack(split, axis=2), ((0, 0), (0, 0), (0, 0), (0, -units % 16), (0, 0)))
    split = [pick(split, (my_x + i) % n_x, 1) for i in range(n_x)]
    split, kv_mine, kv_got = after((split, kv_mine, kv_got))
    split = [split[0]] + [hop(split[i], dx=i) for i in range(1, n_x)]

    kv_chip = jnp.concatenate([kv_mine, kv_got], axis=0)
    q_source, kv_chip = after((queries, kv_chip))
    q_mine, q_other = [lax.dynamic_slice_in_dim(q_source, c * width, width, 1) for c in (my_c, 1 - my_c)]
    q_chip = [q_mine, hop(q_other, dc=1)]

    own_weights, other_weights = [w_gate, w_up, w_down], []
    own_weights, q_chip = after((own_weights, q_chip))
    kv_blocks, state = [], None

    def attend(s, state):
        return attention_call(where, n_z, s, prompt_lengths, q_chip, kv_blocks[s], state)

    newest = kv_chip
    for s in range(n_z):
        kv_blocks.append([newest] + [hop(newest, dx=i) for i in range(1, n_x)])
        onward = hop(newest, dz=1) if s < n_z - 1 else None
        if s == 0:
            split, onward, q_chip = after((split, onward, q_chip))
            split = jnp.stack(split, axis=1)
            turned = [pick(split, (my_z + i) % n_z, 0) for i in range(n_z)]
        elif s == 1:
            near = hop(turned[1], dz=1)
            kv_blocks[0], near, onward, other_weights = after((kv_blocks[0], near, onward, other_weights))
        elif s < n_z - 1:
            state = attend(0, state)
            far = hop(turned[3], dz=3)
            kv_blocks, state, far, onward, other_weights = after((kv_blocks, state, far, onward, other_weights))
        else:
            for i in range(1, n_z - 1):
                state = attend(i, state)
            middle = hop(turned[2], dz=2)
            kv_blocks[s], state, other_weights = after((kv_blocks[s], state, other_weights))
        if s < len(own_weights):
            source, onward = after((own_weights[s], onward))
            other_weights.append(hop(source, dc=1))
        newest = onward
    state = attend(n_z - 1, state)
    attn_mine, attn_other, log_mine, log_other = state
    attn_got = hop(attn_other, dc=1)
    hidden, rows = norm_call(
        where, attn_mine, attn_got, residual, norm_gain.reshape(1, D), expert_ids, router_logits
    )

    def across_x(outs):
        return [hop(outs[i], dx=-i) for i in range(1, n_x)]

    row_blocks, sums = [], []

    def with_shared(s):
        outs = shared_call(row_blocks[s], sums[s], shared)
        return outs[0], [hop(outs[i], dx=-i) for i in range(1, n_x)]

    def experts_of(s):
        return experts_call(where, n_z, row_blocks[s], held_weights, held_done)

    newest, weights = after((rows, own_weights + other_weights))
    for s in range(n_z):
        if s < n_z - 1:
            blocks = [newest] + [hop(newest, dx=i) for i in range(1, n_x)]
            onward = hop(newest, dz=1)
        else:
            blocks = [newest] + [hop(b, dz=1) for b in row_blocks[-1][1:]]
        if s == 0:
            shared = stack_call([turned[0], near, middle, far])
            shared, weights = after((shared, weights))
            shared_near = hop(shared, dc=1)
            shared_far = [hop_group(shared, i) for i in range(1, n_groups)]
            *held_weights, held_done = hold_call(weights)
            blocks, onward, held_done, shared_near = after((blocks, onward, held_done, shared_near))
        elif s < n_z - 1:
            sums.append(experts_call(where, n_z, row_blocks[s - 1], held_weights, held_done))
            if s == 1:
                blocks, onward, sums, shared_far = after((blocks, onward, sums, shared_far))
                parts = [[shared, shared_near]] + [[p, hop(p, dc=1)] for p in shared_far]
            else:
                parts, sums = after((parts, sums))
                shared = assemble_call(where, parts)
                mine_1, back_1 = with_shared(1)
                blocks, onward, mine_1 = after((blocks, onward, mine_1))
        row_blocks.append(blocks)
        newest = onward
    mine_1, row_blocks[2] = after((mine_1, row_blocks[2]))
    sums.append(experts_of(2))
    mine_2, back_2 = with_shared(2)
    mine_1, back_1, mine_2 = after((mine_1, back_1, mine_2))
    total = sum_call([mine_1] + back_1)
    total, row_blocks[3] = after((total, row_blocks[3]))
    from_above = hop(total, dz=-1)
    sums.append(experts_of(3))
    mine_3, back_3 = with_shared(3)
    mine_2, back_2, mine_3, from_above = after((mine_2, back_2, mine_3, from_above))
    total = sum_call([mine_2] + back_2)
    total, sums[0] = after((total, sums[0]))
    from_below = hop(total, dz=1)
    mine_0, back_0 = with_shared(0)
    mine_3, back_3, from_below, mine_0 = after((mine_3, back_3, from_below, mine_0))
    from_below = hop(sum_call([mine_3] + back_3 + [from_below]), dz=1)

    pages_dev = token_rows // PAGE
    own_pages = keys_then_values.reshape(pages_dev, PAGE, keys_then_values.shape[1])
    own_pages, log_other, mine_0 = after((own_pages, log_other, mine_0))
    page_sources = [own_pages] + [hop_group(own_pages, i) for i in range(1, n_groups)]
    log_got = hop(log_other, dc=1)
    kv_cache = pages_call(where, n_columns, page_table, page_sources)
    log_totals = log_call(where, log_mine, log_got)

    layer_out = hidden
    for term in [mine_0] + back_0 + [from_above, from_below]:
        layer_out = layer_out + term.astype(jnp.float32)
    layer_out = layer_out.astype(jnp.bfloat16)
    return (layer_out, kv_cache, log_totals)


def solution(mesh):
    placed = (
        P(("req", "exp"), None),
        P(("req", "exp"), None),
        P(("req", "exp"), None),
        P(),
        P("req", None),
        P(("req", "exp"), None),
        P(("req", "exp"), None),
        P("exp", None, None),
        P("exp", None, None),
        P("exp", None, None),
        P("exp", "req"),
        P("exp", "req"),
        P("exp", "req"),
        P(),
    )
    return jax.shard_map(
        on_device,
        mesh=mesh,
        in_specs=placed,
        out_specs=(P(("req", "exp"), None), P(("req", "exp"), None, None), P(None, ("req", "exp"))),
        check_vma=False,
    )
```

```python
import functools
import math

import jax
import jax.numpy as jnp
from jax import lax
from jax.experimental import pallas as pl
from jax.experimental.pallas import tpu as pltpu
from jax.sharding import PartitionSpec as P

D = 2048
QUERY_HEADS = 16
KEY_VALUE_HEADS = 4
HEAD_SIZE = 128
TOPK = 6
PAGE = 16
CORES = 2
Z_SIZE = 4

large_negative = -1e30
eps_norm = 1e-06
SMALL_LIMIT = 14 * 1024 * 1024
EXPERT_LIMIT = 8 * 1024 * 1024
ASSEMBLE_LIMIT = 2 * 1024 * 1024
HOLD_LIMIT = 16 * 1024 * 1024
LANES = 128
SHARE_LANES = 32
SMALL_COST = pl.CostEstimate(flops=1000, bytes_accessed=1000, transcendentals=0)
SCORE_SCALE = HEAD_SIZE ** (-0.5)
EXP2_SCALE = SCORE_SCALE * math.log2(math.e)


def place_of(n_x, z, x, c):
    return (z * n_x + x) * CORES + c


def source_of(where_ref, n_z, n_x, s, i, parity):
    z = lax.rem(where_ref[1] + n_z - s, n_z)
    x = lax.rem(where_ref[2] + n_x - i, n_x)
    return place_of(n_x, z, x, lax.rem(where_ref[3] + parity, CORES))


def attention_kernel(first, last, n_z, n_x, s, *refs):
    refs = list(refs)
    where_ref, lengths_ref = refs[:2]
    n_blocks = n_x
    queries = refs[2 : 2 + CORES]
    blocks = refs[2 + CORES : 2 + CORES + n_blocks]
    refs = refs[2 + CORES + n_blocks :]
    if not first:
        acc_in, max_in, sum_in = refs[:3]
        refs = refs[3:]
    rows = queries[0].shape[0]
    kv_heads = KEY_VALUE_HEADS // CORES
    heads = QUERY_HEADS // KEY_VALUE_HEADS
    wide = CORES * rows
    iota = lax.broadcasted_iota(jnp.int32, (1, rows), 1)
    query_pos = jnp.concatenate(
        [source_of(where_ref, n_z, n_x, 0, 0, i) * rows + iota for i in range(CORES)], axis=1
    )
    start = jnp.zeros((1, wide), jnp.int32)
    end = jnp.int32(0)
    for i in range(lengths_ref.shape[1]):
        end = end + lengths_ref[0, i]
        start = start + jnp.where(query_pos >= end, lengths_ref[0, i], 0)
    biases = []
    for j in range(n_blocks * CORES):
        key_pos = source_of(where_ref, n_z, n_x, s, j // CORES, j % CORES) * rows
        key_pos = key_pos + lax.broadcasted_iota(jnp.int32, (rows, wide), 0)
        visible = (key_pos >= start) & (key_pos <= query_pos)
        biases.append(jnp.where(visible, 0.0, large_negative))
    bias = jnp.concatenate(biases, axis=0)
    bias = jnp.concatenate([bias] * heads, axis=1)
    for h in range(kv_heads):
        columns = slice(h * HEAD_SIZE, (h + 1) * HEAD_SIZE)
        value_columns = slice((kv_heads + h) * HEAD_SIZE, (kv_heads + h + 1) * HEAD_SIZE)
        keys = jnp.concatenate([b[:, columns] for b in blocks], axis=0)
        values = jnp.concatenate([b[:, value_columns] for b in blocks], axis=0)
        query = jnp.concatenate(
            [
                q[:, (h * heads + g) * HEAD_SIZE : (h * heads + g + 1) * HEAD_SIZE]
                for g in range(heads)
                for q in queries
            ],
            axis=0,
        )
        scores = lax.dot_general(keys, query, (((1,), (1,)), ((), ())), preferred_element_type=jnp.float32)
        scores = scores + bias
        new_max = jnp.max(scores, axis=0, keepdims=True)
        if not first:
            old_max = max_in[h : h + 1, :]
            new_max = jnp.maximum(new_max, old_max)
            fade = jnp.exp2((old_max - new_max) * EXP2_SCALE)
        terms = jnp.exp2((scores - new_max) * EXP2_SCALE)
        total = jnp.sum(terms, axis=0, keepdims=True)
        mixed = lax.dot_general(
            values, terms.astype(jnp.bfloat16), (((0,), (0,)), ((), ())), preferred_element_type=jnp.float32
        )
        if not first:
            total = total + fade * sum_in[h : h + 1, :]
            mixed = mixed + fade * acc_in[h]
        if last:
            mixed = mixed / total
            log_row = new_max * SCORE_SCALE + jnp.log(total)
            for g in range(heads):
                for i in range(CORES):
                    part = slice(g * wide + i * rows, g * wide + (i + 1) * rows)
                    at = h * heads + g
                    refs[i][:, at * HEAD_SIZE : (at + 1) * HEAD_SIZE] = mixed[:, part].T.astype(jnp.bfloat16)
                    refs[CORES + i][at : at + 1, :] = log_row[:, part]
        else:
            refs[0][h] = mixed
            refs[1][h : h + 1, :] = new_max
            refs[2][h : h + 1, :] = total


def attention_call(where, n_z, s, lengths, queries, blocks, state):
    rows, columns = queries[0].shape
    last = s == n_z - 1
    kv_heads = KEY_VALUE_HEADS // CORES
    wide = CORES * rows * (QUERY_HEADS // KEY_VALUE_HEADS)
    vmem, smem = pl.BlockSpec(memory_space=pltpu.VMEM), pl.BlockSpec(memory_space=pltpu.SMEM)
    operands = [where, lengths, *queries, *blocks] + ([] if state is None else list(state))
    if last:
        outs = [jax.ShapeDtypeStruct((rows, columns), jnp.bfloat16)] * CORES
        outs += [jax.ShapeDtypeStruct((QUERY_HEADS // CORES, rows), jnp.float32)] * CORES
    else:
        outs = [jax.ShapeDtypeStruct((kv_heads, HEAD_SIZE, wide), jnp.float32)]
        outs += [jax.ShapeDtypeStruct((kv_heads, wide), jnp.float32)] * 2
    keys = sum(b.shape[0] for b in blocks)
    return pl.pallas_call(
        functools.partial(attention_kernel, state is None, last, n_z, len(blocks), s),
        out_shape=outs,
        in_specs=[smem, smem] + [vmem] * (len(operands) - 2),
        out_specs=[vmem] * len(outs),
        compiler_params=pltpu.CompilerParams(vmem_limit_bytes=SMALL_LIMIT),
        cost_estimate=SMALL_COST,
    )(*operands)


def norm_kernel(where_ref, mine_ref, other_ref, residual_ref, gain_ref, ids_ref, logits_ref, hidden_out, rows_out):
    width = mine_ref.shape[1]
    squares = 0.0
    for i, part in enumerate((mine_ref, other_ref)):
        span = pl.ds(pl.multiple_of(lax.rem(where_ref[3] + i, CORES) * width, width), width)
        hidden = residual_ref[:, span].astype(jnp.float32) + part[...].astype(jnp.float32)
        hidden_out[:, span] = hidden
        squares = squares + jnp.sum(hidden * hidden, axis=-1, keepdims=True)
    scale_rows = lax.rsqrt(squares / D + eps_norm)
    rows_out[:, :D] = (hidden_out[...] * scale_rows * gain_ref[...].astype(jnp.float32)).astype(jnp.bfloat16)
    logits = logits_ref[...]
    terms = jnp.exp(logits - jnp.max(logits, axis=1, keepdims=True))
    route = terms / jnp.sum(terms, axis=1, keepdims=True)
    lanes = lax.broadcasted_iota(jnp.int32, (ids_ref.shape[0], LANES), 1)
    shares = jnp.zeros(lanes.shape, jnp.float32)
    for k in range(TOPK):
        shares = shares + jnp.where(lanes % SHARE_LANES == ids_ref[:, k : k + 1], route[:, k : k + 1], 0.0)
    high = shares.astype(jnp.bfloat16).astype(jnp.float32)
    rows = shares.shape[0]
    earlier = lax.broadcasted_iota(jnp.int32, (rows, rows), 1) < lax.broadcasted_iota(jnp.int32, (rows, rows), 0)
    earlier = jnp.where(earlier, 1.0, 0.0).astype(jnp.bfloat16)
    chosen = jnp.where(shares != 0.0, 1.0, 0.0).astype(jnp.bfloat16)
    rank = jnp.dot(earlier, chosen, preferred_element_type=jnp.float32)
    rest = jnp.where(lanes < 2 * SHARE_LANES, shares - high, rank)
    rows_out[:, D:] = jnp.where(lanes < SHARE_LANES, high, rest).astype(jnp.bfloat16)


def norm_call(where, mine, other, residual, gain, ids, logits):
    vmem, smem = pl.BlockSpec(memory_space=pltpu.VMEM), pl.BlockSpec(memory_space=pltpu.SMEM)
    rows = residual.shape[0]
    return pl.pallas_call(
        norm_kernel,
        out_shape=[
            jax.ShapeDtypeStruct((rows, D), jnp.float32),
            jax.ShapeDtypeStruct((rows, D + LANES), jnp.bfloat16),
        ],
        in_specs=[smem] + [vmem] * 6,
        out_specs=[vmem] * 2,
        compiler_params=pltpu.CompilerParams(vmem_limit_bytes=SMALL_LIMIT),
    )(where, mine, other, residual, gain, ids, logits)


def pieces_of(width, step):
    return [(at, min(step, width - at)) for at in range(0, width, step)]


def silu(value):
    return value / (1.0 + jnp.exp(-value))


def hold_kernel(n, *refs):
    done_ref, sems = refs[2 * n], refs[2 * n + 1]
    done_ref[...] = jnp.zeros_like(done_ref)
    copies = [pltpu.make_async_copy(refs[i].at[0], refs[n + i], sems.at[i]) for i in range(n)]
    for copy in copies:
        copy.start()
    for copy in copies:
        copy.wait()


def hold_call(arrays):
    n = len(arrays)
    return pl.pallas_call(
        functools.partial(hold_kernel, n),
        out_shape=[pltpu.VMEM(a.shape[1:], a.dtype) for a in arrays] + [jax.ShapeDtypeStruct((8, 128), jnp.float32)],
        in_specs=[pl.BlockSpec(memory_space=pltpu.HBM)] * n,
        out_specs=[pl.BlockSpec(memory_space=pltpu.VMEM)] * (n + 1),
        scratch_shapes=[pltpu.SemaphoreType.DMA((n,))],
        compiler_params=pltpu.CompilerParams(vmem_limit_bytes=HOLD_LIMIT),
        cost_estimate=SMALL_COST,
    )(*arrays)


def stack_kernel(n, *refs):
    out_ref, sems = refs[n], refs[n + 1]
    copies = [pltpu.make_async_copy(refs[i], out_ref.at[i], sems.at[i]) for i in range(n)]
    for copy in copies:
        copy.start()
    for copy in copies:
        copy.wait()


def stack_call(arrays):
    n = len(arrays)
    return pl.pallas_call(
        functools.partial(stack_kernel, n),
        out_shape=jax.ShapeDtypeStruct((n,) + arrays[0].shape, arrays[0].dtype),
        in_specs=[pl.BlockSpec(memory_space=pl.ANY)] * n,
        out_specs=pl.BlockSpec(memory_space=pl.ANY),
        scratch_shapes=[pltpu.SemaphoreType.DMA((n,))],
        compiler_params=pltpu.CompilerParams(vmem_limit_bytes=ASSEMBLE_LIMIT),
        cost_estimate=SMALL_COST,
    )(*arrays)


def log_kernel(where_ref, mine_ref, other_ref, out_ref):
    rows = mine_ref.shape[0]
    for i, part in enumerate((mine_ref, other_ref)):
        at = lax.rem(where_ref[3] + i, CORES) * rows
        out_ref[pl.ds(pl.multiple_of(at, rows), rows), :] = part[...]


def log_call(where, mine, other):
    vmem, smem = pl.BlockSpec(memory_space=pltpu.VMEM), pl.BlockSpec(memory_space=pltpu.SMEM)
    return pl.pallas_call(
        log_kernel,
        out_shape=jax.ShapeDtypeStruct((CORES * mine.shape[0], mine.shape[1]), jnp.float32),
        in_specs=[smem, vmem, vmem],
        out_specs=vmem,
        compiler_params=pltpu.CompilerParams(vmem_limit_bytes=ASSEMBLE_LIMIT),
        cost_estimate=SMALL_COST,
    )(where, mine, other)


def assemble_kernel(n_z, n_x, parities, n, where_ref, *refs):
    out_ref, sems = refs[n], refs[n + 1]
    units, width = refs[0].shape[3:]
    copies = []
    for k in range(n):
        for s in range(n_z):
            for i in range(n_x):
                source = source_of(where_ref, n_z, n_x, s, i, k % parities)
                lanes = pl.ds(pl.multiple_of(source // (CORES // parities) * width, LANES), width)
                target = out_ref.at[:, pl.ds(k // parities * units, units), lanes]
                copies.append(pltpu.make_async_copy(refs[k].at[s, i], target, sems.at[len(copies)]))
    for copy in copies:
        copy.start()
    for copy in copies:
        copy.wait()


def assemble_call(where, parts):
    n_z, n_x, three, units, width = parts[0][0].shape
    parities = len(parts[0])
    if width < LANES:
        parities, width = 1, CORES * width
        flip = where[3] == 0
        parts = [[jnp.where(flip, jnp.concatenate(p, axis=-1), jnp.concatenate(p[::-1], axis=-1))] for p in parts]
    operands = [a for p in parts for a in p]
    n = len(operands)
    return pl.pallas_call(
        functools.partial(assemble_kernel, n_z, n_x, parities, n),
        out_shape=pltpu.VMEM((three, len(parts) * units, D), operands[0].dtype),
        in_specs=[pl.BlockSpec(memory_space=pltpu.SMEM)] + [pl.BlockSpec(memory_space=pl.ANY)] * n,
        out_specs=pl.BlockSpec(memory_space=pltpu.VMEM),
        scratch_shapes=[pltpu.SemaphoreType.DMA((n * n_z * n_x,))],
        compiler_params=pltpu.CompilerParams(vmem_limit_bytes=ASSEMBLE_LIMIT),
        cost_estimate=SMALL_COST,
    )(where, *operands)


def experts_kernel(n_z, n_blocks, slots, up_step, down_step, *refs):
    where_ref = refs[0]
    x_in = refs[1 : 1 + n_blocks]
    refs = refs[1 + n_blocks :]
    experts = [refs[3 * e : 3 * e + 3] for e in range(CORES)]
    refs = refs[3 * CORES + 1 :]
    outs, x_scr, act_scr = refs[:n_blocks], refs[n_blocks], refs[n_blocks + 1]
    rows = x_in[0].shape[0]
    units = act_scr.shape[2]
    lane = lax.broadcasted_iota(jnp.int32, (rows, LANES), 1)
    mine = [source_of(where_ref, n_z, n_blocks, 0, 0, e) for e in range(CORES)]
    scales, puts = [[] for _ in mine], []
    for j in range(n_blocks):
        shares = x_in[j][:, D:]
        picks = []
        for e in range(CORES):
            weight = jnp.where((lane % SHARE_LANES == mine[e]) & (lane < 2 * SHARE_LANES), shares.astype(jnp.float32), 0.0)
            chosen = jnp.where(jnp.sum(weight, axis=1, keepdims=True) != 0.0, 1.0, 0.0)
            rank = jnp.where(lane == 2 * SHARE_LANES + mine[e], shares.astype(jnp.float32), 0.0)
            rank = jnp.sum(rank, axis=1, keepdims=True)
            picks.append(jnp.where(rank == lane.astype(jnp.float32), chosen, 0.0))
        puts.append(jnp.concatenate([pick[:, :slots] for pick in picks], axis=1).astype(jnp.bfloat16))
        take = jnp.concatenate([pick.T[:slots] for pick in picks], axis=0).astype(jnp.bfloat16)
        taken = jnp.dot(take, x_in[j][:, :D], preferred_element_type=jnp.float32).astype(jnp.bfloat16)
        taken_shares = jnp.dot(take, shares, preferred_element_type=jnp.float32)
        for e in range(CORES):
            part = slice(e * slots, (e + 1) * slots)
            x_scr[e, j * slots : (j + 1) * slots, :] = taken[part]
            own = lane[:slots]
            own = (own % SHARE_LANES == mine[e]) & (own < 2 * SHARE_LANES)
            scales[e].append(jnp.sum(jnp.where(own, taken_shares[part], 0.0), axis=1, keepdims=True))
    for e in range(CORES):
        x = x_scr[e]
        scale = jnp.concatenate(scales[e], axis=0)
        for at, size in pieces_of(units, up_step):
            gate = jnp.dot(x, experts[e][0][:, at : at + size], preferred_element_type=jnp.float32)
            up = jnp.dot(x, experts[e][1][:, at : at + size], preferred_element_type=jnp.float32)
            act_scr[e, :, at : at + size] = (silu(gate) * up * scale).astype(jnp.bfloat16)
    for at, size in pieces_of(D, down_step):
        parts = [
            jnp.dot(act_scr[e], experts[e][2][:, at : at + size], preferred_element_type=jnp.float32).astype(jnp.bfloat16)
            for e in range(CORES)
        ]
        for j in range(n_blocks):
            both = jnp.concatenate([part[j * slots : (j + 1) * slots] for part in parts], axis=0)
            outs[j][:, at : at + size] = jnp.dot(puts[j], both, preferred_element_type=jnp.float32).astype(jnp.bfloat16)


def experts_call(where, n_z, blocks, weights, held_done):
    rows, n_blocks = blocks[0].shape[0], len(blocks)
    units = weights[0].shape[1]
    experts = n_z * n_blocks * CORES
    capacity = min(rows, 3 * rows * TOPK // (2 * experts))
    slots = capacity + -capacity % 16
    vmem, smem = pl.BlockSpec(memory_space=pltpu.VMEM), pl.BlockSpec(memory_space=pltpu.SMEM)
    return pl.pallas_call(
        functools.partial(experts_kernel, n_z, n_blocks, slots, 512, 512),
        out_shape=[jax.ShapeDtypeStruct((rows, D), jnp.bfloat16)] * n_blocks,
        in_specs=[smem] + [vmem] * (n_blocks + len(weights)) + [pl.BlockSpec(memory_space=pl.ANY)],
        out_specs=[vmem] * n_blocks,
        scratch_shapes=[
            pltpu.VMEM((CORES, n_blocks * slots, D), jnp.bfloat16),
            pltpu.VMEM((CORES, n_blocks * slots, units), jnp.bfloat16),
        ],
        compiler_params=pltpu.CompilerParams(vmem_limit_bytes=EXPERT_LIMIT),
        cost_estimate=SMALL_COST,
    )(where, *blocks, *weights, held_done)


def shared_kernel(n_blocks, pieces, down_step, *refs):
    x_in, sums_in = refs[:n_blocks], refs[n_blocks : 2 * n_blocks]
    shared_ref = refs[2 * n_blocks]
    outs = refs[2 * n_blocks + 1 :]
    rows = x_in[0].shape[0]
    x = jnp.concatenate([x[:, :D] for x in x_in], axis=0)
    across = (((1,), (1,)), ((), ()))
    gate = lax.dot_general(x, shared_ref[0], across, preferred_element_type=jnp.float32)
    up = lax.dot_general(x, shared_ref[1], across, preferred_element_type=jnp.float32)
    act = (silu(gate) * up).astype(jnp.bfloat16)
    for at, size in pieces_of(D, down_step):
        part = jnp.dot(act, shared_ref[2, :, at : at + size], preferred_element_type=jnp.float32)
        for j in range(n_blocks):
            total = part[j * rows : (j + 1) * rows, :] + sums_in[j][:, at : at + size].astype(jnp.float32)
            if j == 0:
                out, start = outs[0], at
            else:
                width = D // pieces
                out, start = outs[1 + (j - 1) * pieces + at // width], at % width
            out[:, start : start + size] = total.astype(jnp.bfloat16)


def shared_call(blocks, sums, shared, pieces):
    rows, n_blocks = blocks[0].shape[0], len(blocks)
    vmem = pl.BlockSpec(memory_space=pltpu.VMEM)
    shapes = [jax.ShapeDtypeStruct((rows, D), jnp.bfloat16)]
    shapes += [jax.ShapeDtypeStruct((rows, D // pieces), jnp.bfloat16)] * ((n_blocks - 1) * pieces)
    outs = pl.pallas_call(
        functools.partial(shared_kernel, n_blocks, pieces, 512),
        out_shape=shapes,
        in_specs=[vmem] * (2 * n_blocks + 1),
        out_specs=[vmem] * len(shapes),
        compiler_params=pltpu.CompilerParams(vmem_limit_bytes=EXPERT_LIMIT),
        cost_estimate=SMALL_COST,
    )(*blocks, *sums, shared)
    return [outs[:1]] + [outs[1 + i * pieces : 1 + (i + 1) * pieces] for i in range(n_blocks - 1)]


def columns_of(ref, half):
    width = D // 2
    return ref[...] if half is None or ref.shape[1] == width else ref[:, half * width : (half + 1) * width]


def sum_kernel(n, half, *refs):
    total = columns_of(refs[0], half).astype(jnp.float32)
    for ref in refs[1:n]:
        total = total + columns_of(ref, half).astype(jnp.float32)
    refs[n][...] = total.astype(jnp.bfloat16)


def sum_call(values, half=None):
    n = len(values)
    vmem = pl.BlockSpec(memory_space=pltpu.VMEM)
    width = D if half is None else D // 2
    return pl.pallas_call(
        functools.partial(sum_kernel, n, half),
        out_shape=jax.ShapeDtypeStruct((values[0].shape[0], width), jnp.bfloat16),
        in_specs=[vmem] * n,
        out_specs=vmem,
        compiler_params=pltpu.CompilerParams(vmem_limit_bytes=EXPERT_LIMIT),
        cost_estimate=SMALL_COST,
    )(*values)


def final_kernel(n, hidden_ref, *refs):
    out_ref = refs[n + 2]
    for half in range(2):
        total = columns_of(hidden_ref, half)
        for ref in refs[:n] + refs[n + half : n + half + 1]:
            total = total + columns_of(ref, half).astype(jnp.float32)
        width = D // 2
        out_ref[:, half * width : (half + 1) * width] = total.astype(jnp.bfloat16)


def final_call(hidden, values, halves):
    n = len(values)
    vmem = pl.BlockSpec(memory_space=pltpu.VMEM)
    return pl.pallas_call(
        functools.partial(final_kernel, n),
        out_shape=jax.ShapeDtypeStruct(hidden.shape, jnp.bfloat16),
        in_specs=[vmem] * (n + 3),
        out_specs=vmem,
        compiler_params=pltpu.CompilerParams(vmem_limit_bytes=SMALL_LIMIT),
        cost_estimate=SMALL_COST,
    )(hidden, *values, *halves)


def pages_kernel(n_groups, n_columns, where_ref, table_ref, *refs):
    sources, out_ref = refs[:n_groups], refs[n_groups]
    pages_dev = out_ref.shape[0]
    first = where_ref[0] * pages_dev
    for i in range(n_groups):
        group = lax.rem(where_ref[4] + n_groups - i, n_groups)
        for j in range(pages_dev):
            slot = table_ref[group, first + j] - (where_ref[4] * n_columns * pages_dev + first)

            @pl.when((slot >= 0) & (slot < pages_dev))
            def _():
                out_ref[slot] = sources[i][j]


def pages_call(where, n_columns, table, sources):
    vmem, smem = pl.BlockSpec(memory_space=pltpu.VMEM), pl.BlockSpec(memory_space=pltpu.SMEM)
    return pl.pallas_call(
        functools.partial(pages_kernel, len(sources), n_columns),
        out_shape=jax.ShapeDtypeStruct(sources[0].shape, jnp.bfloat16),
        in_specs=[smem, smem] + [vmem] * len(sources),
        out_specs=vmem,
        compiler_params=pltpu.CompilerParams(vmem_limit_bytes=SMALL_LIMIT),
    )(where, table, *sources)


def on_device(
    queries,
    keys_then_values,
    residual,
    norm_gain,
    prompt_lengths,
    expert_ids,
    router_logits,
    w_gate,
    w_up,
    w_down,
    w_shared_gate,
    w_shared_up,
    w_shared_down,
    page_table,
):
    token_rows = queries.shape[0]
    n_groups = lax.axis_size("req")
    n_columns = lax.axis_size("exp")
    column = lax.axis_index("exp")
    my_group = lax.axis_index("req")
    n_z, n_x = Z_SIZE, n_columns // (Z_SIZE * CORES)
    my_z, my_x, my_c = column // (n_x * CORES), (column // CORES) % n_x, column % CORES
    where = jnp.stack([column, my_z, my_x, my_c, my_group]).astype(jnp.int32)
    after = lax.optimization_barrier

    def hop(value, dz=0, dx=0, dc=0, wrap=True):
        pairs = [
            (place_of(n_x, z, x, c), place_of(n_x, (z + dz) % n_z, (x + dx) % n_x, (c + dc) % CORES))
            for z in range(n_z)
            for x in range(n_x)
            for c in range(CORES)
            if wrap or z + dz < n_z
        ]
        return lax.ppermute(value, "exp", pairs)

    def hop_group(value, i):
        return lax.ppermute(value, "req", [(g, (g + i) % n_groups) for g in range(n_groups)])

    def across_x(value):
        return [value] + [hop(value, dx=i) for i in range(1, n_x)]

    def pick(value, at, axis):
        return lax.dynamic_index_in_dim(value, at, axis, keepdims=False)

    width = D // CORES
    kv_width = KEY_VALUE_HEADS // CORES * HEAD_SIZE
    kv_mine, kv_other = [
        jnp.concatenate(
            [
                lax.dynamic_slice_in_dim(keys_then_values, at + c * kv_width, kv_width, 1)
                for at in (0, KEY_VALUE_HEADS * HEAD_SIZE)
            ],
            axis=1,
        )
        for c in (my_c, 1 - my_c)
    ]
    kv_got = hop(kv_other, dc=1)

    units = w_shared_gate.shape[1] // (n_z * n_x)
    split = [w.T.reshape(n_z, n_x, units, w.shape[0]) for w in (w_shared_gate, w_shared_up, w_shared_down)]
    split = jnp.pad(jnp.stack(split, axis=2), ((0, 0), (0, 0), (0, 0), (0, -units % 16), (0, 0)))
    split = [pick(split, (my_x + i) % n_x, 1) for i in range(n_x)]
    split, kv_mine, kv_got = after((split, kv_mine, kv_got))
    split = [split[0]] + [hop(split[i], dx=i) for i in range(1, n_x)]

    kv_chip = jnp.concatenate([kv_mine, kv_got], axis=0)
    q_source, kv_chip = after((queries, kv_chip))
    q_mine, q_other = [lax.dynamic_slice_in_dim(q_source, c * width, width, 1) for c in (my_c, 1 - my_c)]
    q_chip = [q_mine, hop(q_other, dc=1)]

    own_weights, other_weights = [w_gate, w_up, w_down], []
    own_weights, q_chip = after((own_weights, q_chip))
    kv_blocks, state = [], None

    def attend(s, state):
        return attention_call(where, n_z, s, prompt_lengths, q_chip, kv_blocks[s], state)

    newest = kv_chip
    for s in range(n_z):
        kv_blocks.append([newest] + [hop(newest, dx=i) for i in range(1, n_x)])
        onward = hop(newest, dz=1, wrap=False) if s < n_z - 1 else None
        if s == 0:
            split, onward, q_chip = after((split, onward, q_chip))
            split = jnp.stack(split, axis=1)
            turned = [pick(split, (my_z + i) % n_z, 0) for i in range(n_z)]
        elif s == 1:
            near = hop(turned[1], dz=1)
            kv_blocks[0], near, onward, other_weights = after((kv_blocks[0], near, onward, other_weights))
        elif s < n_z - 1:
            state = attend(0, state)
            far = hop(turned[3], dz=3)
            kv_blocks, state, far, onward, other_weights = after((kv_blocks, state, far, onward, other_weights))
        else:
            for i in range(1, n_z - 1):
                state = attend(i, state)
            middle = hop(turned[2], dz=2)
            kv_blocks[s], state, other_weights = after((kv_blocks[s], state, other_weights))
        if s < len(own_weights):
            source, onward = after((own_weights[s], onward))
            other_weights.append(hop(source, dc=1))
        newest = onward
    state = attend(n_z - 1, state)
    attn_mine, attn_other, log_mine, log_other = state
    attn_got = hop(attn_other, dc=1)
    hidden, rows = norm_call(
        where, attn_mine, attn_got, residual, norm_gain.reshape(1, D), expert_ids, router_logits
    )

    def across_x(outs):
        return [hop(outs[i], dx=-i) for i in range(1, n_x)]

    row_blocks, sums = [], []

    def with_shared(s, pieces=1):
        outs = shared_call(row_blocks[s], sums[s], shared, pieces)
        moving = [[hop(part, dx=-i) for part in outs[i]] for i in range(1, n_x)]
        return outs[0][0], [list(one) for one in zip(*moving)] if pieces > 1 else [one[0] for one in moving]

    def experts_of(s):
        return experts_call(where, n_z, row_blocks[s], held_weights, held_done)

    newest, weights = after((rows, own_weights + other_weights))
    for s in range(n_z):
        if s < n_z - 1:
            blocks = [newest] + [hop(newest, dx=i) for i in range(1, n_x)]
            onward = hop(newest, dz=1)
        else:
            blocks = [newest] + [hop(b, dz=1) for b in row_blocks[-1][1:]]
        if s == 0:
            shared = stack_call([turned[0], near, middle, far])
            shared, weights = after((shared, weights))
            shared_near = hop(shared, dc=1)
            shared_far = [hop_group(shared, i) for i in range(1, n_groups)]
            *held_weights, held_done = hold_call(weights)
            blocks, onward, held_done, shared_near = after((blocks, onward, held_done, shared_near))
        elif s < n_z - 1:
            sums.append(experts_call(where, n_z, row_blocks[s - 1], held_weights, held_done))
            if s == 1:
                log_got = hop(log_other, dc=1)
                shared_far, sums, log_got = after((shared_far, sums, log_got))
                log_totals = log_call(where, log_mine, log_got)
                parts = [[shared, shared_near]] + [[p, hop(p, dc=1)] for p in shared_far]
                blocks, onward, sums, log_totals = after((blocks, onward, sums, log_totals))
            else:
                parts, sums = after((parts, sums))
                shared = assemble_call(where, parts)
                mine_1, back_1 = with_shared(1)
                blocks, onward, mine_1 = after((blocks, onward, mine_1))
        row_blocks.append(blocks)
        newest = onward
    mine_1, row_blocks[2] = after((mine_1, row_blocks[2]))
    sums.append(experts_of(2))
    mine_2, back_2 = with_shared(2)
    own_pages = keys_then_values.reshape(token_rows // PAGE, PAGE, keys_then_values.shape[1])
    own_pages, mine_2 = after((own_pages, mine_2))
    page_sources = [own_pages] + [hop_group(own_pages, i) for i in range(1, n_groups)]
    mine_1, back_1, mine_2 = after((mine_1, back_1, mine_2))
    total = sum_call([mine_1] + back_1)
    total, row_blocks[3] = after((total, row_blocks[3]))
    from_above = hop(total, dz=-1)
    sums.append(experts_of(3))
    mine_2, back_2, from_above, sums[3], page_sources = after((mine_2, back_2, from_above, sums[3], page_sources))
    total = sum_call([mine_2] + back_2)
    total, sums[3] = after((total, sums[3]))
    from_below = hop(total, dz=1)
    mine_3, back_3 = with_shared(3, 2)
    mine_3, sums[0] = after((mine_3, sums[0]))
    mine_0, back_0 = with_shared(0)
    page_sources, mine_0 = after((page_sources, mine_0))
    kv_cache = pages_call(where, n_columns, page_table, page_sources)
    mine_3, back_3, from_below, mine_0, kv_cache = after((mine_3, back_3, from_below, mine_0, kv_cache))
    halves = [hop(sum_call([mine_3] + back_3[h] + [from_below], h), dz=1) for h in range(2)]

    layer_out = final_call(hidden, [mine_0] + back_0 + [from_above], halves)
    return (layer_out, kv_cache, log_totals)


def solution(mesh):
    placed = (
        P(("req", "exp"), None),
        P(("req", "exp"), None),
        P(("req", "exp"), None),
        P(),
        P("req", None),
        P(("req", "exp"), None),
        P(("req", "exp"), None),
        P("exp", None, None),
        P("exp", None, None),
        P("exp", None, None),
        P("exp", "req"),
        P("exp", "req"),
        P("exp", "req"),
        P(),
    )
    return jax.shard_map(
        on_device,
        mesh=mesh,
        in_specs=placed,
        out_specs=(P(("req", "exp"), None), P(("req", "exp"), None, None), P(None, ("req", "exp"))),
        check_vma=False,
    )
```

```python
import functools
import math

import jax
import jax.numpy as jnp
from jax import lax
from jax.experimental import pallas as pl
from jax.experimental.pallas import tpu as pltpu
from jax.sharding import PartitionSpec as P

D = 2048
QUERY_HEADS = 16
KEY_VALUE_HEADS = 4
HEAD_SIZE = 128
TOPK = 6
PAGE = 16
CORES = 2
Z_SIZE = 4

large_negative = -1e30
eps_norm = 1e-06
SMALL_LIMIT = 14 * 1024 * 1024
EXPERT_LIMIT = 8 * 1024 * 1024
ASSEMBLE_LIMIT = 2 * 1024 * 1024
HOLD_LIMIT = 16 * 1024 * 1024
LANES = 128
SHARE_LANES = 32
SMALL_COST = pl.CostEstimate(flops=1000, bytes_accessed=1000, transcendentals=0)
SCORE_SCALE = HEAD_SIZE ** (-0.5)
EXP2_SCALE = SCORE_SCALE * math.log2(math.e)


def place_of(n_x, z, x, c):
    return (z * n_x + x) * CORES + c


def source_of(where_ref, n_z, n_x, s, i, parity):
    z = lax.rem(where_ref[1] + n_z - s, n_z)
    x = lax.rem(where_ref[2] + n_x - i, n_x)
    return place_of(n_x, z, x, lax.rem(where_ref[3] + parity, CORES))


def attention_kernel(first, last, n_z, n_x, s, *refs):
    refs = list(refs)
    where_ref, lengths_ref = refs[:2]
    n_blocks = n_x
    queries = refs[2 : 2 + CORES]
    blocks = refs[2 + CORES : 2 + CORES + n_blocks]
    refs = refs[2 + CORES + n_blocks :]
    if not first:
        acc_in, max_in, sum_in = refs[:3]
        refs = refs[3:]
    rows = queries[0].shape[0]
    kv_heads = KEY_VALUE_HEADS // CORES
    heads = QUERY_HEADS // KEY_VALUE_HEADS
    wide = CORES * rows
    iota = lax.broadcasted_iota(jnp.int32, (1, rows), 1)
    query_pos = jnp.concatenate(
        [source_of(where_ref, n_z, n_x, 0, 0, i) * rows + iota for i in range(CORES)], axis=1
    )
    start = jnp.zeros((1, wide), jnp.int32)
    end = jnp.int32(0)
    for i in range(lengths_ref.shape[1]):
        end = end + lengths_ref[0, i]
        start = start + jnp.where(query_pos >= end, lengths_ref[0, i], 0)
    biases = []
    for j in range(n_blocks * CORES):
        key_pos = source_of(where_ref, n_z, n_x, s, j // CORES, j % CORES) * rows
        key_pos = key_pos + lax.broadcasted_iota(jnp.int32, (rows, wide), 0)
        visible = (key_pos >= start) & (key_pos <= query_pos)
        biases.append(jnp.where(visible, 0.0, large_negative))
    bias = jnp.concatenate(biases, axis=0)
    bias = jnp.concatenate([bias] * heads, axis=1)
    for h in range(kv_heads):
        columns = slice(h * HEAD_SIZE, (h + 1) * HEAD_SIZE)
        value_columns = slice((kv_heads + h) * HEAD_SIZE, (kv_heads + h + 1) * HEAD_SIZE)
        keys = jnp.concatenate([b[:, columns] for b in blocks], axis=0)
        values = jnp.concatenate([b[:, value_columns] for b in blocks], axis=0)
        query = jnp.concatenate(
            [
                q[:, (h * heads + g) * HEAD_SIZE : (h * heads + g + 1) * HEAD_SIZE]
                for g in range(heads)
                for q in queries
            ],
            axis=0,
        )
        scores = lax.dot_general(keys, query, (((1,), (1,)), ((), ())), preferred_element_type=jnp.float32)
        scores = scores + bias
        new_max = jnp.max(scores, axis=0, keepdims=True)
        if not first:
            old_max = max_in[h : h + 1, :]
            new_max = jnp.maximum(new_max, old_max)
            fade = jnp.exp2((old_max - new_max) * EXP2_SCALE)
        terms = jnp.exp2((scores - new_max) * EXP2_SCALE)
        total = jnp.sum(terms, axis=0, keepdims=True)
        mixed = lax.dot_general(
            values, terms.astype(jnp.bfloat16), (((0,), (0,)), ((), ())), preferred_element_type=jnp.float32
        )
        if not first:
            total = total + fade * sum_in[h : h + 1, :]
            mixed = mixed + fade * acc_in[h]
        if last:
            mixed = mixed / total
            log_row = new_max * SCORE_SCALE + jnp.log(total)
            for g in range(heads):
                for i in range(CORES):
                    part = slice(g * wide + i * rows, g * wide + (i + 1) * rows)
                    at = h * heads + g
                    refs[i][:, at * HEAD_SIZE : (at + 1) * HEAD_SIZE] = mixed[:, part].T.astype(jnp.bfloat16)
                    refs[CORES + i][at : at + 1, :] = log_row[:, part]
        else:
            refs[0][h] = mixed
            refs[1][h : h + 1, :] = new_max
            refs[2][h : h + 1, :] = total


def attention_call(where, n_z, s, lengths, queries, blocks, state):
    rows, columns = queries[0].shape
    last = s == n_z - 1
    kv_heads = KEY_VALUE_HEADS // CORES
    wide = CORES * rows * (QUERY_HEADS // KEY_VALUE_HEADS)
    vmem, smem = pl.BlockSpec(memory_space=pltpu.VMEM), pl.BlockSpec(memory_space=pltpu.SMEM)
    operands = [where, lengths, *queries, *blocks] + ([] if state is None else list(state))
    if last:
        outs = [jax.ShapeDtypeStruct((rows, columns), jnp.bfloat16)] * CORES
        outs += [jax.ShapeDtypeStruct((QUERY_HEADS // CORES, rows), jnp.float32)] * CORES
    else:
        outs = [jax.ShapeDtypeStruct((kv_heads, HEAD_SIZE, wide), jnp.float32)]
        outs += [jax.ShapeDtypeStruct((kv_heads, wide), jnp.float32)] * 2
    keys = sum(b.shape[0] for b in blocks)
    return pl.pallas_call(
        functools.partial(attention_kernel, state is None, last, n_z, len(blocks), s),
        out_shape=outs,
        in_specs=[smem, smem] + [vmem] * (len(operands) - 2),
        out_specs=[vmem] * len(outs),
        compiler_params=pltpu.CompilerParams(vmem_limit_bytes=SMALL_LIMIT),
        cost_estimate=SMALL_COST,
    )(*operands)


def norm_kernel(where_ref, mine_ref, other_ref, residual_ref, gain_ref, ids_ref, logits_ref, hidden_out, rows_out):
    width = mine_ref.shape[1]
    squares = 0.0
    for i, part in enumerate((mine_ref, other_ref)):
        span = pl.ds(pl.multiple_of(lax.rem(where_ref[3] + i, CORES) * width, width), width)
        hidden = residual_ref[:, span].astype(jnp.float32) + part[...].astype(jnp.float32)
        hidden_out[:, span] = hidden
        squares = squares + jnp.sum(hidden * hidden, axis=-1, keepdims=True)
    scale_rows = lax.rsqrt(squares / D + eps_norm)
    rows_out[:, :D] = (hidden_out[...] * scale_rows * gain_ref[...].astype(jnp.float32)).astype(jnp.bfloat16)
    logits = logits_ref[...]
    terms = jnp.exp(logits - jnp.max(logits, axis=1, keepdims=True))
    route = terms / jnp.sum(terms, axis=1, keepdims=True)
    lanes = lax.broadcasted_iota(jnp.int32, (ids_ref.shape[0], LANES), 1)
    shares = jnp.zeros(lanes.shape, jnp.float32)
    for k in range(TOPK):
        shares = shares + jnp.where(lanes % SHARE_LANES == ids_ref[:, k : k + 1], route[:, k : k + 1], 0.0)
    high = shares.astype(jnp.bfloat16).astype(jnp.float32)
    rows = shares.shape[0]
    earlier = lax.broadcasted_iota(jnp.int32, (rows, rows), 1) < lax.broadcasted_iota(jnp.int32, (rows, rows), 0)
    earlier = jnp.where(earlier, 1.0, 0.0).astype(jnp.bfloat16)
    chosen = jnp.where(shares != 0.0, 1.0, 0.0).astype(jnp.bfloat16)
    rank = jnp.dot(earlier, chosen, preferred_element_type=jnp.float32)
    rest = jnp.where(lanes < 2 * SHARE_LANES, shares - high, rank)
    rows_out[:, D:] = jnp.where(lanes < SHARE_LANES, high, rest).astype(jnp.bfloat16)


def norm_call(where, mine, other, residual, gain, ids, logits):
    vmem, smem = pl.BlockSpec(memory_space=pltpu.VMEM), pl.BlockSpec(memory_space=pltpu.SMEM)
    rows = residual.shape[0]
    return pl.pallas_call(
        norm_kernel,
        out_shape=[
            jax.ShapeDtypeStruct((rows, D), jnp.float32),
            jax.ShapeDtypeStruct((rows, D + LANES), jnp.bfloat16),
        ],
        in_specs=[smem] + [vmem] * 6,
        out_specs=[vmem] * 2,
        compiler_params=pltpu.CompilerParams(vmem_limit_bytes=SMALL_LIMIT),
    )(where, mine, other, residual, gain, ids, logits)


def pieces_of(width, step):
    return [(at, min(step, width - at)) for at in range(0, width, step)]


def silu(value):
    return value / (1.0 + jnp.exp(-value))


def hold_kernel(n, *refs):
    done_ref, sems = refs[2 * n], refs[2 * n + 1]
    done_ref[...] = jnp.zeros_like(done_ref)
    copies = [pltpu.make_async_copy(refs[i].at[0], refs[n + i], sems.at[i]) for i in range(n)]
    for copy in copies:
        copy.start()
    for copy in copies:
        copy.wait()


def hold_call(arrays):
    n = len(arrays)
    return pl.pallas_call(
        functools.partial(hold_kernel, n),
        out_shape=[pltpu.VMEM(a.shape[1:], a.dtype) for a in arrays] + [jax.ShapeDtypeStruct((8, 128), jnp.float32)],
        in_specs=[pl.BlockSpec(memory_space=pltpu.HBM)] * n,
        out_specs=[pl.BlockSpec(memory_space=pltpu.VMEM)] * (n + 1),
        scratch_shapes=[pltpu.SemaphoreType.DMA((n,))],
        compiler_params=pltpu.CompilerParams(vmem_limit_bytes=HOLD_LIMIT),
        cost_estimate=SMALL_COST,
    )(*arrays)


def stack_kernel(n, *refs):
    out_ref, sems = refs[n], refs[n + 1]
    copies = [pltpu.make_async_copy(refs[i], out_ref.at[i], sems.at[i]) for i in range(n)]
    for copy in copies:
        copy.start()
    for copy in copies:
        copy.wait()


def stack_call(arrays):
    n = len(arrays)
    return pl.pallas_call(
        functools.partial(stack_kernel, n),
        out_shape=jax.ShapeDtypeStruct((n,) + arrays[0].shape, arrays[0].dtype),
        in_specs=[pl.BlockSpec(memory_space=pl.ANY)] * n,
        out_specs=pl.BlockSpec(memory_space=pl.ANY),
        scratch_shapes=[pltpu.SemaphoreType.DMA((n,))],
        compiler_params=pltpu.CompilerParams(vmem_limit_bytes=ASSEMBLE_LIMIT),
        cost_estimate=SMALL_COST,
    )(*arrays)


def log_kernel(where_ref, mine_ref, other_ref, out_ref):
    rows = mine_ref.shape[0]
    for i, part in enumerate((mine_ref, other_ref)):
        at = lax.rem(where_ref[3] + i, CORES) * rows
        out_ref[pl.ds(pl.multiple_of(at, rows), rows), :] = part[...]


def log_call(where, mine, other):
    vmem, smem = pl.BlockSpec(memory_space=pltpu.VMEM), pl.BlockSpec(memory_space=pltpu.SMEM)
    return pl.pallas_call(
        log_kernel,
        out_shape=jax.ShapeDtypeStruct((CORES * mine.shape[0], mine.shape[1]), jnp.float32),
        in_specs=[smem, vmem, vmem],
        out_specs=vmem,
        compiler_params=pltpu.CompilerParams(vmem_limit_bytes=ASSEMBLE_LIMIT),
        cost_estimate=SMALL_COST,
    )(where, mine, other)


def assemble_kernel(n_z, n_x, parities, n, where_ref, *refs):
    out_ref, sems = refs[n], refs[n + 1]
    units, width = refs[0].shape[3:]
    copies = []
    for k in range(n):
        for s in range(n_z):
            for i in range(n_x):
                source = source_of(where_ref, n_z, n_x, s, i, k % parities)
                lanes = pl.ds(pl.multiple_of(source // (CORES // parities) * width, LANES), width)
                target = out_ref.at[:, pl.ds(k // parities * units, units), lanes]
                copies.append(pltpu.make_async_copy(refs[k].at[s, i], target, sems.at[len(copies)]))
    for copy in copies:
        copy.start()
    for copy in copies:
        copy.wait()


def assemble_call(where, parts):
    n_z, n_x, three, units, width = parts[0][0].shape
    parities = len(parts[0])
    if width < LANES:
        parities, width = 1, CORES * width
        flip = where[3] == 0
        parts = [[jnp.where(flip, jnp.concatenate(p, axis=-1), jnp.concatenate(p[::-1], axis=-1))] for p in parts]
    operands = [a for p in parts for a in p]
    n = len(operands)
    return pl.pallas_call(
        functools.partial(assemble_kernel, n_z, n_x, parities, n),
        out_shape=pltpu.VMEM((three, len(parts) * units, D), operands[0].dtype),
        in_specs=[pl.BlockSpec(memory_space=pltpu.SMEM)] + [pl.BlockSpec(memory_space=pl.ANY)] * n,
        out_specs=pl.BlockSpec(memory_space=pltpu.VMEM),
        scratch_shapes=[pltpu.SemaphoreType.DMA((n * n_z * n_x,))],
        compiler_params=pltpu.CompilerParams(vmem_limit_bytes=ASSEMBLE_LIMIT),
        cost_estimate=SMALL_COST,
    )(where, *operands)


def experts_kernel(n_z, n_blocks, slots, up_step, down_step, *refs):
    where_ref = refs[0]
    x_in = refs[1 : 1 + n_blocks]
    refs = refs[1 + n_blocks :]
    experts = [refs[3 * e : 3 * e + 3] for e in range(CORES)]
    refs = refs[3 * CORES + 1 :]
    outs, x_scr, act_scr = refs[:n_blocks], refs[n_blocks], refs[n_blocks + 1]
    rows = x_in[0].shape[0]
    units = act_scr.shape[2]
    lane = lax.broadcasted_iota(jnp.int32, (rows, LANES), 1)
    mine = [source_of(where_ref, n_z, n_blocks, 0, 0, e) for e in range(CORES)]
    scales, puts = [[] for _ in mine], []
    for j in range(n_blocks):
        shares = x_in[j][:, D:]
        picks = []
        for e in range(CORES):
            weight = jnp.where((lane % SHARE_LANES == mine[e]) & (lane < 2 * SHARE_LANES), shares.astype(jnp.float32), 0.0)
            chosen = jnp.where(jnp.sum(weight, axis=1, keepdims=True) != 0.0, 1.0, 0.0)
            rank = jnp.where(lane == 2 * SHARE_LANES + mine[e], shares.astype(jnp.float32), 0.0)
            rank = jnp.sum(rank, axis=1, keepdims=True)
            picks.append(jnp.where(rank == lane.astype(jnp.float32), chosen, 0.0))
        puts.append(jnp.concatenate([pick[:, :slots] for pick in picks], axis=1).astype(jnp.bfloat16))
        take = jnp.concatenate([pick.T[:slots] for pick in picks], axis=0).astype(jnp.bfloat16)
        taken = jnp.dot(take, x_in[j][:, :D], preferred_element_type=jnp.float32).astype(jnp.bfloat16)
        taken_shares = jnp.dot(take, shares, preferred_element_type=jnp.float32)
        for e in range(CORES):
            part = slice(e * slots, (e + 1) * slots)
            x_scr[e, j * slots : (j + 1) * slots, :] = taken[part]
            own = lane[:slots]
            own = (own % SHARE_LANES == mine[e]) & (own < 2 * SHARE_LANES)
            scales[e].append(jnp.sum(jnp.where(own, taken_shares[part], 0.0), axis=1, keepdims=True))
    for e in range(CORES):
        x = x_scr[e]
        scale = jnp.concatenate(scales[e], axis=0)
        for at, size in pieces_of(units, up_step):
            gate = jnp.dot(x, experts[e][0][:, at : at + size], preferred_element_type=jnp.float32)
            up = jnp.dot(x, experts[e][1][:, at : at + size], preferred_element_type=jnp.float32)
            act_scr[e, :, at : at + size] = (silu(gate) * up * scale).astype(jnp.bfloat16)
    for at, size in pieces_of(D, down_step):
        parts = [
            jnp.dot(act_scr[e], experts[e][2][:, at : at + size], preferred_element_type=jnp.float32).astype(jnp.bfloat16)
            for e in range(CORES)
        ]
        for j in range(n_blocks):
            both = jnp.concatenate([part[j * slots : (j + 1) * slots] for part in parts], axis=0)
            outs[j][:, at : at + size] = jnp.dot(puts[j], both, preferred_element_type=jnp.float32).astype(jnp.bfloat16)


def experts_call(where, n_z, blocks, weights, held_done):
    rows, n_blocks = blocks[0].shape[0], len(blocks)
    units = weights[0].shape[1]
    experts = n_z * n_blocks * CORES
    capacity = min(rows, 3 * rows * TOPK // (2 * experts))
    slots = capacity + -capacity % 16
    vmem, smem = pl.BlockSpec(memory_space=pltpu.VMEM), pl.BlockSpec(memory_space=pltpu.SMEM)
    return pl.pallas_call(
        functools.partial(experts_kernel, n_z, n_blocks, slots, 512, 512),
        out_shape=[jax.ShapeDtypeStruct((rows, D), jnp.bfloat16)] * n_blocks,
        in_specs=[smem] + [vmem] * (n_blocks + len(weights)) + [pl.BlockSpec(memory_space=pl.ANY)],
        out_specs=[vmem] * n_blocks,
        scratch_shapes=[
            pltpu.VMEM((CORES, n_blocks * slots, D), jnp.bfloat16),
            pltpu.VMEM((CORES, n_blocks * slots, units), jnp.bfloat16),
        ],
        compiler_params=pltpu.CompilerParams(vmem_limit_bytes=EXPERT_LIMIT),
        cost_estimate=SMALL_COST,
    )(where, *blocks, *weights, held_done)


def shared_kernel(n_blocks, pieces, down_step, *refs):
    x_in, sums_in = refs[:n_blocks], refs[n_blocks : 2 * n_blocks]
    shared_ref = refs[2 * n_blocks]
    outs = refs[2 * n_blocks + 1 :]
    rows = x_in[0].shape[0]
    x = jnp.concatenate([x[:, :D] for x in x_in], axis=0)
    across = (((1,), (1,)), ((), ()))
    gate = lax.dot_general(x, shared_ref[0], across, preferred_element_type=jnp.float32)
    up = lax.dot_general(x, shared_ref[1], across, preferred_element_type=jnp.float32)
    act = (silu(gate) * up).astype(jnp.bfloat16)
    for at, size in pieces_of(D, down_step):
        part = jnp.dot(act, shared_ref[2, :, at : at + size], preferred_element_type=jnp.float32)
        for j in range(n_blocks):
            total = part[j * rows : (j + 1) * rows, :] + sums_in[j][:, at : at + size].astype(jnp.float32)
            if j == 0:
                out, start = outs[0], at
            else:
                width = D // pieces
                out, start = outs[1 + (j - 1) * pieces + at // width], at % width
            out[:, start : start + size] = total.astype(jnp.bfloat16)


def shared_call(blocks, sums, shared, pieces):
    rows, n_blocks = blocks[0].shape[0], len(blocks)
    vmem = pl.BlockSpec(memory_space=pltpu.VMEM)
    shapes = [jax.ShapeDtypeStruct((rows, D), jnp.bfloat16)]
    shapes += [jax.ShapeDtypeStruct((rows, D // pieces), jnp.bfloat16)] * ((n_blocks - 1) * pieces)
    outs = pl.pallas_call(
        functools.partial(shared_kernel, n_blocks, pieces, 512),
        out_shape=shapes,
        in_specs=[vmem] * (2 * n_blocks + 1),
        out_specs=[vmem] * len(shapes),
        compiler_params=pltpu.CompilerParams(vmem_limit_bytes=EXPERT_LIMIT),
        cost_estimate=SMALL_COST,
    )(*blocks, *sums, shared)
    return [outs[:1]] + [outs[1 + i * pieces : 1 + (i + 1) * pieces] for i in range(n_blocks - 1)]


def columns_of(ref, half):
    width = D // 2
    return ref[...] if half is None or ref.shape[1] == width else ref[:, half * width : (half + 1) * width]


def sum_kernel(n, half, *refs):
    total = columns_of(refs[0], half).astype(jnp.float32)
    for ref in refs[1:n]:
        total = total + columns_of(ref, half).astype(jnp.float32)
    refs[n][...] = total.astype(jnp.bfloat16)


def sum_call(values, half=None):
    n = len(values)
    vmem = pl.BlockSpec(memory_space=pltpu.VMEM)
    width = D if half is None else D // 2
    return pl.pallas_call(
        functools.partial(sum_kernel, n, half),
        out_shape=jax.ShapeDtypeStruct((values[0].shape[0], width), jnp.bfloat16),
        in_specs=[vmem] * n,
        out_specs=vmem,
        compiler_params=pltpu.CompilerParams(vmem_limit_bytes=EXPERT_LIMIT),
        cost_estimate=SMALL_COST,
    )(*values)


def final_kernel(n, hidden_ref, *refs):
    out_ref = refs[n + 2]
    for half in range(2):
        total = columns_of(hidden_ref, half)
        for ref in refs[:n] + refs[n + half : n + half + 1]:
            total = total + columns_of(ref, half).astype(jnp.float32)
        width = D // 2
        out_ref[:, half * width : (half + 1) * width] = total.astype(jnp.bfloat16)


def final_call(hidden, values, halves):
    n = len(values)
    vmem = pl.BlockSpec(memory_space=pltpu.VMEM)
    return pl.pallas_call(
        functools.partial(final_kernel, n),
        out_shape=jax.ShapeDtypeStruct(hidden.shape, jnp.bfloat16),
        in_specs=[vmem] * (n + 3),
        out_specs=vmem,
        compiler_params=pltpu.CompilerParams(vmem_limit_bytes=SMALL_LIMIT),
        cost_estimate=SMALL_COST,
    )(hidden, *values, *halves)


def pages_kernel(n_groups, n_columns, where_ref, table_ref, *refs):
    sources, out_ref = refs[:n_groups], refs[n_groups]
    pages_dev = out_ref.shape[0]
    first = where_ref[0] * pages_dev
    for i in range(n_groups):
        group = lax.rem(where_ref[4] + n_groups - i, n_groups)
        for j in range(pages_dev):
            slot = table_ref[group, first + j] - (where_ref[4] * n_columns * pages_dev + first)

            @pl.when((slot >= 0) & (slot < pages_dev))
            def _():
                out_ref[slot] = sources[i][j]


def pages_call(where, n_columns, table, sources):
    vmem, smem = pl.BlockSpec(memory_space=pltpu.VMEM), pl.BlockSpec(memory_space=pltpu.SMEM)
    return pl.pallas_call(
        functools.partial(pages_kernel, len(sources), n_columns),
        out_shape=jax.ShapeDtypeStruct(sources[0].shape, jnp.bfloat16),
        in_specs=[smem, smem] + [vmem] * len(sources),
        out_specs=vmem,
        compiler_params=pltpu.CompilerParams(vmem_limit_bytes=SMALL_LIMIT),
    )(where, table, *sources)


def on_device(
    queries,
    keys_then_values,
    residual,
    norm_gain,
    prompt_lengths,
    expert_ids,
    router_logits,
    w_gate,
    w_up,
    w_down,
    w_shared_gate,
    w_shared_up,
    w_shared_down,
    page_table,
):
    token_rows = queries.shape[0]
    n_groups = lax.axis_size("req")
    n_columns = lax.axis_size("exp")
    column = lax.axis_index("exp")
    my_group = lax.axis_index("req")
    n_z, n_x = Z_SIZE, n_columns // (Z_SIZE * CORES)
    my_z, my_x, my_c = column // (n_x * CORES), (column // CORES) % n_x, column % CORES
    where = jnp.stack([column, my_z, my_x, my_c, my_group]).astype(jnp.int32)
    after = lax.optimization_barrier

    def hop(value, dz=0, dx=0, dc=0, wrap=True):
        pairs = [
            (place_of(n_x, z, x, c), place_of(n_x, (z + dz) % n_z, (x + dx) % n_x, (c + dc) % CORES))
            for z in range(n_z)
            for x in range(n_x)
            for c in range(CORES)
            if wrap or z + dz < n_z
        ]
        return lax.ppermute(value, "exp", pairs)

    def hop_group(value, i):
        return lax.ppermute(value, "req", [(g, (g + i) % n_groups) for g in range(n_groups)])

    def across_x(value):
        return [value] + [hop(value, dx=i) for i in range(1, n_x)]

    def pick(value, at, axis):
        return lax.dynamic_index_in_dim(value, at, axis, keepdims=False)

    width = D // CORES
    kv_width = KEY_VALUE_HEADS // CORES * HEAD_SIZE
    kv_mine, kv_other = [
        jnp.concatenate(
            [
                lax.dynamic_slice_in_dim(keys_then_values, at + c * kv_width, kv_width, 1)
                for at in (0, KEY_VALUE_HEADS * HEAD_SIZE)
            ],
            axis=1,
        )
        for c in (my_c, 1 - my_c)
    ]
    kv_got = hop(kv_other, dc=1)

    units = w_shared_gate.shape[1] // (n_z * n_x)
    split = [w.T.reshape(n_z, n_x, units, w.shape[0]) for w in (w_shared_gate, w_shared_up, w_shared_down)]
    split = jnp.pad(jnp.stack(split, axis=2), ((0, 0), (0, 0), (0, 0), (0, -units % 16), (0, 0)))
    split = [pick(split, (my_x + i) % n_x, 1) for i in range(n_x)]
    split, kv_mine, kv_got = after((split, kv_mine, kv_got))
    split = [split[0]] + [hop(split[i], dx=i) for i in range(1, n_x)]

    kv_chip = jnp.concatenate([kv_mine, kv_got], axis=0)
    q_source, kv_chip = after((queries, kv_chip))
    q_mine, q_other = [lax.dynamic_slice_in_dim(q_source, c * width, width, 1) for c in (my_c, 1 - my_c)]
    q_chip = [q_mine, hop(q_other, dc=1)]

    own_weights, other_weights = [w_gate, w_up, w_down], []
    own_weights, q_chip = after((own_weights, q_chip))
    kv_blocks, state = [], None

    def attend(s, state):
        return attention_call(where, n_z, s, prompt_lengths, q_chip, kv_blocks[s], state)

    newest = kv_chip
    for s in range(n_z):
        onward = hop(newest, dz=1, wrap=False) if s < n_z - 1 else None
        kv_blocks.append([newest] + [hop(newest, dx=i) for i in range(1, n_x)])
        if s == 0:
            split, onward, q_chip = after((split, onward, q_chip))
            split = jnp.stack(split, axis=1)
            turned = [pick(split, (my_z + i) % n_z, 0) for i in range(n_z)]
        elif s == 1:
            near = hop(turned[1], dz=1)
            kv_blocks, near, onward, other_weights = after((kv_blocks, near, onward, other_weights))
        elif s < n_z - 1:
            state = attend(0, state)
            far = hop(turned[3], dz=3)
            kv_blocks, state, far, onward, other_weights = after((kv_blocks, state, far, onward, other_weights))
        else:
            for i in range(1, n_z - 1):
                state = attend(i, state)
            middle = hop(turned[2], dz=2)
            kv_blocks[s], state, other_weights = after((kv_blocks[s], state, other_weights))
        if s < len(own_weights):
            source, onward = after((own_weights[s], onward))
            other_weights.append(hop(source, dc=1))
        newest = onward
    state = attend(n_z - 1, state)
    attn_mine, attn_other, log_mine, log_other = state
    attn_got = hop(attn_other, dc=1)
    hidden, rows = norm_call(
        where, attn_mine, attn_got, residual, norm_gain.reshape(1, D), expert_ids, router_logits
    )

    def across_x(outs):
        return [hop(outs[i], dx=-i) for i in range(1, n_x)]

    row_blocks, sums = [], []

    def with_shared(s, pieces=1):
        outs = shared_call(row_blocks[s], sums[s], shared, pieces)
        moving = [[hop(part, dx=-i) for part in outs[i]] for i in range(1, n_x)]
        return outs[0][0], [list(one) for one in zip(*moving)] if pieces > 1 else [one[0] for one in moving]

    def experts_of(s):
        return experts_call(where, n_z, row_blocks[s], held_weights, held_done)

    newest, weights = after((rows, own_weights + other_weights))
    for s in range(n_z):
        if s < n_z - 1:
            onward = hop(newest, dz=1)
            blocks = [newest] + [hop(newest, dx=i) for i in range(1, n_x)]
        else:
            blocks = [newest] + [hop(b, dz=1) for b in row_blocks[-1][1:]]
        if s == 0:
            shared = stack_call([turned[0], near, middle, far])
            shared, weights = after((shared, weights))
            shared_near = hop(shared, dc=1)
            shared_far = [hop_group(shared, i) for i in range(1, n_groups)]
            *held_weights, held_done = hold_call(weights)
            onward, blocks, held_done, shared_near = after((onward, blocks, held_done, shared_near))
        elif s < n_z - 1:
            sums.append(experts_call(where, n_z, row_blocks[s - 1], held_weights, held_done))
            if s == 1:
                log_got = hop(log_other, dc=1)
                shared_far, sums, log_got = after((shared_far, sums, log_got))
                log_totals = log_call(where, log_mine, log_got)
                parts = [[shared, shared_near]] + [[p, hop(p, dc=1)] for p in shared_far]
                onward, blocks, sums, log_totals = after((onward, blocks, sums, log_totals))
            else:
                parts, sums = after((parts, sums))
                shared = assemble_call(where, parts)
                mine_1, back_1 = with_shared(1)
                onward, blocks, mine_1 = after((onward, blocks, mine_1))
        row_blocks.append(blocks)
        newest = onward
    mine_1, row_blocks[2] = after((mine_1, row_blocks[2]))
    sums.append(experts_of(2))
    mine_2, back_2 = with_shared(2)
    own_pages = keys_then_values.reshape(token_rows // PAGE, PAGE, keys_then_values.shape[1])
    own_pages, mine_2 = after((own_pages, mine_2))
    page_sources = [own_pages] + [hop_group(own_pages, i) for i in range(1, n_groups)]
    mine_1, back_1, mine_2 = after((mine_1, back_1, mine_2))
    total = sum_call([mine_1] + back_1)
    total, row_blocks[3] = after((total, row_blocks[3]))
    from_above = hop(total, dz=-1)
    sums.append(experts_of(3))
    mine_2, back_2, from_above, sums[3], page_sources = after((mine_2, back_2, from_above, sums[3], page_sources))
    total = sum_call([mine_2] + back_2)
    total, sums[3] = after((total, sums[3]))
    from_below = hop(total, dz=1)
    mine_3, back_3 = with_shared(3, 2)
    mine_3, sums[0] = after((mine_3, sums[0]))
    outs_0 = shared_call(row_blocks[0], sums[0], shared, 1)
    page_sources, outs_0 = after((page_sources, outs_0))
    kv_cache = pages_call(where, n_columns, page_table, page_sources)
    mine_3, back_3[0], from_below, outs_0, kv_cache = after((mine_3, back_3[0], from_below, outs_0, kv_cache))
    total = sum_call([mine_3] + back_3[0] + [from_below], 0)
    total, back_3[1], outs_0 = after((total, back_3[1], outs_0))
    halves = [hop(total, dz=1), hop(sum_call([mine_3] + back_3[1] + [from_below], 1), dz=1)]
    mine_0, back_0 = outs_0[0][0], [hop(outs_0[i][0], dx=-i) for i in range(1, n_x)]

    layer_out = final_call(hidden, [mine_0] + back_0 + [from_above], halves)
    return (layer_out, kv_cache, log_totals)


def solution(mesh):
    placed = (
        P(("req", "exp"), None),
        P(("req", "exp"), None),
        P(("req", "exp"), None),
        P(),
        P("req", None),
        P(("req", "exp"), None),
        P(("req", "exp"), None),
        P("exp", None, None),
        P("exp", None, None),
        P("exp", None, None),
        P("exp", "req"),
        P("exp", "req"),
        P("exp", "req"),
        P(),
    )
    return jax.shard_map(
        on_device,
        mesh=mesh,
        in_specs=placed,
        out_specs=(P(("req", "exp"), None), P(("req", "exp"), None, None), P(None, ("req", "exp"))),
        check_vma=False,
    )
```
